32 devices in a mesh: ctx: 8 (over z, y), fsdp: 4 (over x, core).
Axes of the slice: x: 2, y: 2, z: 4, core: 2. Of those that a mesh axis runs over, the one named last changes fastest.
Arguments:
- inputs: bfloat16 [16, 1024, 640], P('fsdp', 'ctx'), may hold values from -6 to 6
- cotangent: bfloat16 [16, 1024, 640], P('fsdp', 'ctx'), may hold values from -6 to 6
- lengths: int32 [16], P('fsdp'), may hold values from 256 to 1024, as said below
- query_weight: bfloat16 [640, 1024], P('fsdp'), may hold values from -0.25 to 0.25
- key_weight: bfloat16 [640, 256], P('fsdp'), may hold values from -0.25 to 0.25
- value_weight: bfloat16 [640, 256], P('fsdp'), may hold values from -0.25 to 0.25
- out_weight: bfloat16 [1024, 640], P('fsdp'), may hold values from -0.1875 to 0.1875
- gate_weight: bfloat16 [640, 2048], P('fsdp'), may hold values from -0.25 to 0.25
- up_weight: bfloat16 [640, 2048], P('fsdp'), may hold values from -0.25 to 0.25
- down_weight: bfloat16 [2048, 640], P('fsdp'), may hold values from -0.125 to 0.125
- pre_attn_gain: bfloat16 [640], P('fsdp'), may hold values from -0.5 to 0.5
- post_attn_gain: bfloat16 [640], P('fsdp'), may hold values from -0.5 to 0.5
- pre_ffw_gain: bfloat16 [640], P('fsdp'), may hold values from -0.5 to 0.5
- post_ffw_gain: bfloat16 [640], P('fsdp'), may hold values from -0.5 to 0.5
- query_gain: bfloat16 [256], P('fsdp'), may hold values from 0 to 0.796875
- key_gain: bfloat16 [256], P('fsdp'), may hold values from 0 to 0.796875
Outputs:
- outputs: bfloat16 [16, 1024, 640], P('fsdp', 'ctx')
- input_grad: bfloat16 [16, 1024, 640], P('fsdp', 'ctx')
- query_weight_grad: float32 [640, 1024], P('fsdp')
- key_weight_grad: float32 [640, 256], P('fsdp')
- value_weight_grad: float32 [640, 256], P('fsdp')
- out_weight_grad: float32 [1024, 640], P('fsdp')
- gate_weight_grad: float32 [640, 2048], P('fsdp')
- up_weight_grad: float32 [640, 2048], P('fsdp')
- down_weight_grad: float32 [2048, 640], P('fsdp')
- pre_attn_gain_grad: float32 [640], P('fsdp')
- post_attn_gain_grad: float32 [640], P('fsdp')
- pre_ffw_gain_grad: float32 [640], P('fsdp')
- post_ffw_gain_grad: float32 [640], P('fsdp')
- query_gain_grad: float32 [256], P('fsdp')
- key_gain_grad: float32 [256], P('fsdp')
The draws below stay inside these ranges and needn't reach their ends.
Inputs may be any that keep to these rules, and one draw needn't show every extreme that they name: Sequence s has its first lengths[s] positions live; later keys are excluded from every softmax. In each aligned block of 4 sequences exactly one, drawn from the seed, has all 1024 positions live.
All inputs are finite; a program needn't handle non-finite values.
Results may differ from the reference program's by a relative error of at most 0.022.
Values may be sent and summed in bfloat16 or wider, within the bound.
A program may use at most 256 MiB of HBM per device.

```python
import jax
import jax.numpy as jnp
from jax import lax

D = 640
HEADS = 4
HEAD_DIM = 256
FF = 2048
SEQ_DEV = 4
SEQS = 16
LENGTH = 1024


def draw_lengths(key, part):
    key = jax.random.fold_in(key, 7)
    base_key, pick_key = jax.random.split(key)
    base_lengths = jax.random.randint(base_key, (SEQS,), LENGTH // 4, LENGTH + 1)
    chosen = jax.random.randint(pick_key, (SEQS // SEQ_DEV,), 0, SEQ_DEV)
    slot_index = jnp.arange(SEQS) % SEQ_DEV
    is_whole = slot_index == jnp.repeat(chosen, SEQ_DEV)
    return jnp.where(is_whole, LENGTH, base_lengths).astype(jnp.int32)


def steps_of(stream_key, dims, cuts, smallest, high):
    def one(dim, blocks):
        steps = jax.random.uniform(jax.random.fold_in(jax.random.fold_in(stream_key, 6), dim), (blocks,), jnp.float32, smallest / len(cuts), high / len(cuts))
        return jnp.repeat(jnp.exp(steps), dims[dim] // blocks).reshape((-1,) + (1,) * (len(dims) - dim - 1))

    level = one(*cuts[0])
    for cut in cuts[1:]:
        level = level * one(*cut)
    return level


def scatter_about(own_key, shape, deviation, most, cuts=(), held_as=jnp.bfloat16):
    drawn = jax.random.normal(own_key, shape, jnp.float32) * deviation
    if len(cuts) > 0:
        drawn = steps_of(own_key, shape, cuts, -0.22, 0.18) * drawn
    return jnp.clip(drawn, min=-most, max=most).astype(held_as)


def setup_inputs(seed: int = 0) -> dict:
    arg_keys = jax.random.split(jax.random.key(seed), 17)
    inputs = scatter_about(arg_keys[0], (SEQS, LENGTH, D), 1.0, 6.0, ((0, 4), (1, 8)))
    cotangent = scatter_about(arg_keys[1], (SEQS, LENGTH, D), 1.0, 6.0, ((0, 4), (1, 8)))
    lengths = draw_lengths(jax.random.fold_in(arg_keys[16], 71), 0)
    query_weight = scatter_about(arg_keys[3], (D, HEADS * HEAD_DIM), D ** -0.5, 0.25, ((0, 4),))
    key_weight = scatter_about(arg_keys[4], (D, HEAD_DIM), D ** -0.5, 0.25, ((0, 4),))
    value_weight = scatter_about(arg_keys[5], (D, HEAD_DIM), D ** -0.5, 0.25, ((0, 4),))
    out_weight = scatter_about(arg_keys[6], (HEADS * HEAD_DIM, D), (HEADS * HEAD_DIM) ** -0.5, 0.1875, ((0, 4),))
    gate_weight = scatter_about(arg_keys[7], (D, FF), D ** -0.5, 0.25, ((0, 4),))
    up_weight = scatter_about(arg_keys[8], (D, FF), D ** -0.5, 0.25, ((0, 4),))
    down_weight = scatter_about(arg_keys[9], (FF, D), FF ** -0.5, 0.125, ((0, 4),))
    pre_attn_gain = jnp.clip(jax.random.uniform(arg_keys[10], (D,), jnp.float32, -0.5, 0.5) * steps_of(arg_keys[10], (D,), ((0, 4),), -0.4, 0.0), -0.5, 0.5).astype(jnp.bfloat16)
    post_attn_gain = jnp.clip(jax.random.uniform(arg_keys[11], (D,), jnp.float32, -0.5, 0.5) * steps_of(arg_keys[11], (D,), ((0, 4),), -0.4, 0.0), -0.5, 0.5).astype(jnp.bfloat16)
    pre_ffw_gain = jnp.clip(jax.random.uniform(arg_keys[12], (D,), jnp.float32, -0.5, 0.5) * steps_of(arg_keys[12], (D,), ((0, 4),), -0.4, 0.0), -0.5, 0.5).astype(jnp.bfloat16)
    post_ffw_gain = jnp.clip(jax.random.uniform(arg_keys[13], (D,), jnp.float32, -0.5, 0.5) * steps_of(arg_keys[13], (D,), ((0, 4),), -0.4, 0.0), -0.5, 0.5).astype(jnp.bfloat16)
    query_gain = jnp.clip(0.796875 * jax.random.uniform(arg_keys[14], (HEAD_DIM,), jnp.float32) ** steps_of(arg_keys[14], (HEAD_DIM,), ((0, 4),), -0.2, 0.2), 0.0, 0.796875).astype(jnp.bfloat16)
    key_gain = jnp.clip(0.796875 * jax.random.uniform(arg_keys[15], (HEAD_DIM,), jnp.float32) ** steps_of(arg_keys[15], (HEAD_DIM,), ((0, 4),), -0.2, 0.2), 0.0, 0.796875).astype(jnp.bfloat16)
    return dict(inputs=inputs, cotangent=cotangent, lengths=lengths, query_weight=query_weight, key_weight=key_weight, value_weight=value_weight, out_weight=out_weight, gate_weight=gate_weight, up_weight=up_weight, down_weight=down_weight, pre_attn_gain=pre_attn_gain, post_attn_gain=post_attn_gain, pre_ffw_gain=pre_ffw_gain, post_ffw_gain=post_ffw_gain, query_gain=query_gain, key_gain=key_gain)


EPSILON = 1e-06
MASKED_SCORE = -1e+30
ROPE_BASE = 1000000.0

@jax.custom_vjp
def low(v):
    return lax.optimization_barrier(v.astype(jnp.bfloat16)).astype(jnp.float32)

@jax.custom_vjp
def low_back(v):
    return v

def low_keep(v):
    return (low(v), None)

def low_pass(kept, grad):
    return (grad,)

def back_keep(v):
    return (v, None)

def back_low(kept, grad):
    return (low(grad),)
low.defvjp(low_keep, low_pass)
low_back.defvjp(back_keep, back_low)

def norm_gain(values, gain_vec):
    return values * lax.rsqrt(lax.optimization_barrier(jnp.mean(values * values, axis=-1, keepdims=True)) + EPSILON) * (1.0 + gain_vec)

def rotate(values, positions):
    half_dim = values.shape[-1] // 2
    inverse = ROPE_BASE ** (-(jnp.arange(half_dim).astype(jnp.float32) * 2.0) / values.shape[-1])
    angles = positions.astype(jnp.float32)[:, None] * inverse[None, :]
    cosine = jnp.cos(angles)[:, None, :]
    sine_part = jnp.sin(angles)[:, None, :]
    first_half = values[..., :half_dim]
    second_half = values[..., half_dim:]
    return jnp.concatenate([first_half * cosine - second_half * sine_part, second_half * cosine + first_half * sine_part], axis=-1)

def product(left, right):
    return jnp.dot(left, right, precision=lax.Precision.HIGHEST, preferred_element_type=jnp.float32)

def attend(query_b, key_b, value_b, live_len):
    seq_len = query_b.shape[0]
    block_rows = min(512, seq_len)
    key_pos = jnp.arange(seq_len).astype(jnp.int32)

    def attend_block(row_begin):
        queries = lax.dynamic_slice_in_dim(query_b, row_begin, block_rows, 0)
        scores = low_back(jnp.einsum('qhd,kd->hqk', queries, key_b, precision=lax.Precision.HIGHEST) * HEAD_DIM ** (-0.5))
        query_pos = row_begin + jnp.arange(block_rows).astype(jnp.int32)
        allowed = (key_pos[None, :] <= query_pos[:, None]) & (key_pos[None, :] < live_len)
        scores = jnp.where(allowed[None], scores, MASKED_SCORE)
        highest = lax.optimization_barrier(jnp.max(scores, axis=-1, keepdims=True))
        weights = jnp.exp(scores - highest)
        total = lax.optimization_barrier(jnp.sum(weights, axis=-1))
        mixed_rows = jnp.einsum('hqk,kd->qhd', low(weights), value_b, precision=lax.Precision.HIGHEST) / jnp.transpose(total)[:, :, None]
        return mixed_rows.reshape(block_rows, -1)
    begins = (jnp.arange(seq_len // block_rows) * block_rows).astype(jnp.int32)
    return lax.map(jax.checkpoint(attend_block), begins).reshape(seq_len, -1)

def layer(hidden_in, live_len, params):
    query_w, key_w, value_w, out_w, gate_w, up_w, down_w, gain_attn_in, gain_attn_out, gain_ffw_in, gain_ffw_out, gain_query, gain_key = params
    seq_len = hidden_in.shape[0]
    positions = jnp.arange(seq_len).astype(jnp.int32)
    attn_in = low(norm_gain(hidden_in, gain_attn_in))
    query_lin = low_back(product(attn_in, query_w)).reshape(seq_len, HEADS, HEAD_DIM)
    key_lin = low_back(product(attn_in, key_w))
    value_b = low(low_back(product(attn_in, value_w)))
    query_b = low(rotate(norm_gain(query_lin, gain_query), positions))
    key_b = low(rotate(norm_gain(key_lin, gain_key)[:, None, :], positions)[:, 0, :])
    attended = attend(query_b, key_b, value_b, live_len)
    attended_b = low(low_back(attended))
    attn_lin = low_back(product(attended_b, out_w))
    middle = hidden_in + norm_gain(attn_lin, gain_attn_out)
    ffw_in = low(norm_gain(middle, gain_ffw_in))
    gate_lin = low_back(product(ffw_in, gate_w))
    up_lin = low_back(product(ffw_in, up_w))
    hidden = low(jax.nn.gelu(gate_lin, approximate=True) * up_lin)
    ffw_out = low_back(product(hidden, down_w))
    return middle + norm_gain(ffw_out, gain_ffw_out)

def reference(inputs, cotangent, lengths, query_weight, key_weight, value_weight, out_weight, gate_weight, up_weight, down_weight, pre_attn_gain, post_attn_gain, pre_ffw_gain, post_ffw_gain, query_gain, key_gain):
    params = tuple((item.astype(jnp.float32) for item in (query_weight, key_weight, value_weight, out_weight, gate_weight, up_weight, down_weight, pre_attn_gain, post_attn_gain, pre_ffw_gain, post_ffw_gain, query_gain, key_gain)))
    checked_layer = jax.checkpoint(layer)

    def forward(hidden_all, weights_all):
        return lax.map(lambda item: checked_layer(item[0], item[1], weights_all), (hidden_all, lengths))
    outputs, pullback = jax.vjp(forward, inputs.astype(jnp.float32), params)
    input_grad, weight_grads = pullback(cotangent.astype(jnp.float32))
    return (outputs.astype(jnp.bfloat16), input_grad.astype(jnp.bfloat16), weight_grads[0], weight_grads[1], weight_grads[2], weight_grads[3], weight_grads[4], weight_grads[5], weight_grads[6], weight_grads[7], weight_grads[8], weight_grads[9], weight_grads[10], weight_grads[11], weight_grads[12])
```

```python
import math

import jax
import jax.numpy as jnp
from jax import lax
from jax.experimental import pallas as pl
from jax.experimental.pallas import tpu as pltpu
from jax.sharding import PartitionSpec as P

EPSILON = 1e-06
MASKED_SCORE = -1e30
ROPE_BASE = 1000000.0


def norm_gain(values, gain_vec):
    return (
        values
        * lax.rsqrt(jnp.mean(values * values, axis=-1, keepdims=True) + EPSILON)
        * (1.0 + gain_vec)
    )


def rotate(values, positions):
    half_dim = values.shape[-1] // 2
    inverse = ROPE_BASE ** (-(jnp.arange(half_dim).astype(jnp.float32) * 2.0) / values.shape[-1])
    angles = positions.astype(jnp.float32)[:, None] * inverse[None, :]
    cosine = jnp.cos(angles)[:, None, :]
    sine_part = jnp.sin(angles)[:, None, :]
    first_half = values[..., :half_dim]
    second_half = values[..., half_dim:]
    return jnp.concatenate(
        [
            first_half * cosine - second_half * sine_part,
            second_half * cosine + first_half * sine_part,
        ],
        axis=-1,
    )


MESH_ID = pl.DeviceIdType.MESH
VMEM_BYTES = 56 * 1024 * 1024


def place():
    ctx = lax.axis_index("ctx")
    fsdp = lax.axis_index("fsdp")
    return lax.rem(ctx, 2), lax.div(ctx, 2), lax.rem(fsdp, 2), lax.div(fsdp, 2)


def device(y, z, core, x):
    return (z * 2 + y, x * 2 + core)


def greet(peers):
    barrier = pltpu.get_barrier_semaphore()
    for peer in peers:
        pl.semaphore_signal(barrier, inc=1, device_id=peer, device_id_type=MESH_ID)
    pl.semaphore_wait(barrier, len(peers))


def reduce_kernel(by_columns, *refs):
    count = len(by_columns)
    grads, gains = refs[:count], refs[count]
    outs, gain_out = refs[count + 1 : 2 * count + 1], refs[2 * count + 1]
    refs = refs[2 * count + 2 :]
    core_in, x_in, y_in, z_in = (refs[i * count : (i + 1) * count] for i in range(4))
    gain_in, gain_sum, send_sem, recv_sem, gain_send, gain_recv = refs[4 * count :]
    y, z, core, x = place()
    core_peer = device(y, z, 1 - core, x)
    x_peer = device(y, z, core, 1 - x)
    y_peer = device(1 - y, z, core, x)
    z_at = [lax.rem(z + hop, 4) for hop in (1, 2, 3)]
    z_peers = [device(y, other, core, x) for other in z_at]
    greet([core_peer, x_peer, y_peer] + z_peers)

    def quarter(item, ref, at):
        if by_columns[item]:
            width = ref.shape[1] // 4
            return ref.at[:, pl.ds(pl.multiple_of(at * width, 128), width)]
        width = ref.shape[0] // 4
        return ref.at[pl.ds(pl.multiple_of(at * width, 16), width), :]

    def copy(item, slot, source, target, peer):
        return pltpu.make_async_remote_copy(
            src_ref=source,
            dst_ref=target,
            send_sem=send_sem.at[item, slot],
            recv_sem=recv_sem.at[item, slot],
            device_id=peer,
            device_id_type=MESH_ID,
        )

    def gain_copy(slot, source, peer):
        return pltpu.make_async_remote_copy(
            src_ref=source,
            dst_ref=gain_in.at[slot],
            send_sem=gain_send.at[slot],
            recv_sem=gain_recv.at[slot],
            device_id=peer,
            device_id_type=MESH_ID,
        )

    def add_rows(target, others):
        rows = target.shape[0]

        @pl.loop(0, rows // 16)
        def _(step):
            span = pl.ds(pl.multiple_of(step * 16, 16), 16)
            total = others[0][span, :].astype(jnp.float32)
            for other in others[1:]:
                total = total + other[span, :].astype(jnp.float32)
            target[span, :] = total.astype(target.dtype)

    copies = [[None] * 10 for _ in range(count)]
    gain_copies = [None] * 6

    def stage_core(item):
        copies[item][0] = copy(item, 0, grads[item].at[:, 1 - core], core_in[item], core_peer)
        copies[item][0].start()

    def stage_x(item):
        copies[item][0].wait_recv()
        for side in range(2):
            for half in range(2):
                target = core_in[item].at[side, half]
                add_rows(target, [target, grads[item].at[side, core, half]])
        copies[item][1] = copy(item, 1, core_in[item].at[1 - x], x_in[item], x_peer)
        copies[item][1].start()

    def stage_y(item):
        copies[item][1].wait_recv()
        for half in range(2):
            target = x_in[item].at[half]
            add_rows(target, [target, core_in[item].at[x, half]])
        copies[item][2] = copy(item, 2, x_in[item].at[1 - y], y_in[item], y_peer)
        copies[item][2].start()

    def stage_z(item):
        copies[item][2].wait_recv()
        add_rows(y_in[item], [y_in[item], x_in[item].at[y]])
        for hop in range(3):
            copies[item][3 + hop] = copy(
                item, 3 + hop, quarter(item, y_in[item], z_at[hop]), z_in[item].at[hop], z_peers[hop]
            )
            copies[item][3 + hop].start()

    def stage_back_z(item):
        for hop in range(3):
            copies[item][3 + hop].wait_recv()
        mine = quarter(item, outs[item].at[y], z)
        add_rows(mine, [quarter(item, y_in[item], z)] + [z_in[item].at[hop] for hop in range(3)])
        for hop in range(3):
            copies[item][6 + hop] = copy(item, 6 + hop, mine, mine, z_peers[hop])
            copies[item][6 + hop].start()

    def stage_back_y(item):
        for hop in range(3):
            copies[item][6 + hop].wait_recv()
        copies[item][9] = copy(item, 9, outs[item].at[y], outs[item].at[y], y_peer)
        copies[item][9].start()

    def gain_step(step):
        if step == 0:
            gain_copies[0] = gain_copy(0, gains, core_peer)
            gain_copies[0].start()
        elif step <= 2:
            gain_copies[step - 1].wait_recv()
            before = gains if step == 1 else gain_sum.at[step - 2]
            gain_sum[step - 1] = before[...] + gain_in[step - 1]
            gain_copies[step] = gain_copy(step, gain_sum.at[step - 1], (x_peer, y_peer)[step - 1])
            gain_copies[step].start()
        elif step == 3:
            gain_copies[2].wait_recv()
            gain_sum[2] = gain_sum[1] + gain_in[2]
            for hop in range(3):
                gain_copies[3 + hop] = gain_copy(3 + hop, gain_sum.at[2], z_peers[hop])
                gain_copies[3 + hop].start()
        elif step == 4:
            for hop in range(3):
                gain_copies[3 + hop].wait_recv()
            gain_out[...] = (gain_sum[2] + gain_in[4]) + (gain_in[3] + gain_in[5])

    for item in range(count):
        stage_core(item)
    stages = (stage_x, stage_y, stage_z, stage_back_z, stage_back_y)
    for tick in range(count + len(stages) - 1):
        for at, stage in enumerate(stages):
            if 0 <= tick - at < count:
                stage(tick - at)
        gain_step(tick)
    for item in range(count):
        copies[item][9].wait_recv()
    for item in range(count):
        for slot in range(10):
            copies[item][slot].wait_send()
    for slot in range(6):
        gain_copies[slot].wait_send()


def reduce_all(grads, by_columns, gains):
    shaped, outs, scratch = [], [], [[], [], [], []]
    for grad, columns_split in zip(grads, by_columns):
        rows, columns = grad.shape[0] // 8, grad.shape[1]
        shaped.append(grad.reshape(2, 2, 2, rows, columns))
        outs.append(jax.ShapeDtypeStruct((2, rows, columns), jnp.bfloat16))
        piece = (rows, columns // 4) if columns_split else (rows // 4, columns)
        scratch[0].append(pltpu.VMEM((2, 2, rows, columns), jnp.bfloat16))
        scratch[1].append(pltpu.VMEM((2, rows, columns), jnp.bfloat16))
        scratch[2].append(pltpu.VMEM((rows, columns), jnp.bfloat16))
        scratch[3].append(pltpu.VMEM((3,) + piece, jnp.bfloat16))
    count = len(grads)
    outs.append(jax.ShapeDtypeStruct(gains.shape, jnp.float32))
    sent = sum(grad.size for grad in grads)

    def kernel(*refs):
        reduce_kernel(by_columns, *refs)

    results = pl.pallas_call(
        kernel,
        out_shape=outs,
        in_specs=[pl.BlockSpec(memory_space=pltpu.VMEM)] * (count + 1),
        out_specs=[pl.BlockSpec(memory_space=pltpu.VMEM)] * (count + 1),
        scratch_shapes=scratch[0]
        + scratch[1]
        + scratch[2]
        + scratch[3]
        + [
            pltpu.VMEM((6,) + gains.shape, jnp.float32),
            pltpu.VMEM((3,) + gains.shape, jnp.float32),
            pltpu.SemaphoreType.DMA((count, 10)),
            pltpu.SemaphoreType.DMA((count, 10)),
            pltpu.SemaphoreType.DMA((6,)),
            pltpu.SemaphoreType.DMA((6,)),
        ],
        compiler_params=pltpu.CompilerParams(
            collective_id=1, has_side_effects=True, vmem_limit_bytes=VMEM_BYTES
        ),
        cost_estimate=pl.CostEstimate(flops=2 * sent, bytes_accessed=4 * sent, transcendentals=0),
        name="reduce_grads",
    )(*shaped, gains)
    return [
        result.reshape(2 * result.shape[1], result.shape[2]) for result in results[:-1]
    ] + [results[-1]]


def gelu_mix(gate_in, up_in):
    return jax.nn.gelu(gate_in, approximate=True) * up_in


def body(
    inputs,
    cotangent,
    lengths,
    query_weight,
    key_weight,
    value_weight,
    out_weight,
    gate_weight,
    up_weight,
    down_weight,
    pre_attn_gain,
    post_attn_gain,
    pre_ffw_gain,
    post_ffw_gain,
    query_gain,
    key_gain,
):
    seq_count, row_count, model_width = inputs.shape
    fast = lax.axis_size("ctx") == 8 and lax.axis_size("fsdp") == 4
    gathered = (
        lax.all_gather(query_weight, "fsdp", axis=0, tiled=True),
        lax.all_gather(key_weight, "fsdp", axis=0, tiled=True),
        lax.all_gather(value_weight, "fsdp", axis=0, tiled=True),
        lax.all_gather(out_weight, "fsdp", axis=0, tiled=True),
        lax.all_gather(gate_weight, "fsdp", axis=0, tiled=True),
        lax.all_gather(up_weight, "fsdp", axis=0, tiled=True),
        lax.all_gather(down_weight, "fsdp", axis=0, tiled=True),
        lax.all_gather(pre_attn_gain, "fsdp", axis=0, tiled=True),
        lax.all_gather(post_attn_gain, "fsdp", axis=0, tiled=True),
        lax.all_gather(pre_ffw_gain, "fsdp", axis=0, tiled=True),
        lax.all_gather(post_ffw_gain, "fsdp", axis=0, tiled=True),
        lax.all_gather(query_gain, "fsdp", axis=0, tiled=True),
        lax.all_gather(key_gain, "fsdp", axis=0, tiled=True),
    )
    (
        query_full,
        key_full,
        value_full,
        out_full,
        gate_full,
        up_full,
        down_full,
        gain_attn_in,
        gain_attn_out,
        gain_ffw_in,
        gain_ffw_out,
        gain_query,
        gain_key,
    ) = gathered
    gain_attn_in = gain_attn_in.astype(jnp.float32)
    gain_attn_out = gain_attn_out.astype(jnp.float32)
    gain_ffw_in = gain_ffw_in.astype(jnp.float32)
    gain_ffw_out = gain_ffw_out.astype(jnp.float32)
    gain_query = gain_query.astype(jnp.float32)
    gain_key = gain_key.astype(jnp.float32)
    head_dim = key_full.shape[1]
    head_count = query_full.shape[1] // head_dim
    seq_len = row_count * lax.axis_size("ctx")
    key_span = math.gcd(512, seq_len)
    att_scale = head_dim ** (-0.5)
    flat_rows = seq_count * row_count
    positions = lax.axis_index("ctx") * row_count + jnp.arange(row_count, dtype=jnp.int32)
    x_flat = inputs.astype(jnp.float32).reshape(flat_rows, model_width)
    attn_in, attn_in_back = jax.vjp(norm_gain, x_flat, gain_attn_in)
    attn_in_b = attn_in.astype(jnp.bfloat16)
    query_lin = jnp.dot(attn_in_b, query_full, preferred_element_type=jnp.float32)
    key_lin = jnp.dot(attn_in_b, key_full, preferred_element_type=jnp.float32)
    value_lin = jnp.dot(attn_in_b, value_full, preferred_element_type=jnp.float32)

    def query_side(lin_values, gain_vec):
        return rotate(
            norm_gain(lin_values.reshape(seq_count, row_count, head_count, head_dim), gain_vec),
            positions,
        )

    def key_side(lin_values, gain_vec):
        return rotate(
            norm_gain(lin_values.reshape(seq_count, row_count, 1, head_dim), gain_vec), positions
        )[:, :, 0, :]

    query_rot, query_side_back = jax.vjp(query_side, query_lin, gain_query)
    key_rot, key_side_back = jax.vjp(key_side, key_lin, gain_key)
    query_b = query_rot.astype(jnp.bfloat16)
    key_b = key_rot.astype(jnp.bfloat16)
    value_b = value_lin.reshape(seq_count, row_count, head_dim).astype(jnp.bfloat16)

    def allowed(key_begin, key_count):
        key_pos = key_begin + jnp.arange(key_count, dtype=jnp.int32)
        causal = key_pos[None, :] <= positions[:, None]
        live = key_pos[None, :] < lengths[:, None]
        return (causal[None] & live[:, None, :])[:, None]

    def raw_scores(key_piece):
        return (
            jnp.einsum("sqhd,skd->shqk", query_b, key_piece, preferred_element_type=jnp.float32)
            * att_scale
        )

    stat_shape = (seq_count, head_count, row_count)
    running_max = jnp.full(stat_shape, MASKED_SCORE, jnp.float32)
    key_piece = lax.all_gather(key_b, "ctx", axis=1, tiled=True)
    value_piece = lax.all_gather(value_b, "ctx", axis=1, tiled=True)
    mask_now = allowed(jnp.int32(0), key_piece.shape[1])
    scores = jnp.where(mask_now, raw_scores(key_piece), MASKED_SCORE)
    new_max = jnp.maximum(running_max, jnp.max(scores, axis=-1))
    weights = jnp.where(mask_now, jnp.exp(scores - new_max[..., None]), 0.0)
    new_sum = jnp.sum(weights, axis=-1)
    new_acc = jnp.einsum(
        "shqk,skd->shqd",
        weights.astype(jnp.bfloat16),
        value_piece,
        preferred_element_type=jnp.float32,
    )
    final_state = (new_max, new_sum, new_acc)
    final_max, final_sum, final_acc = final_state
    attended = final_acc / final_sum[..., None]
    log_total = final_max + jnp.log(final_sum)
    attended_b = (
        attended.transpose(0, 2, 1, 3)
        .reshape(flat_rows, head_count * head_dim)
        .astype(jnp.bfloat16)
    )
    attn_lin = jnp.dot(attended_b, out_full, preferred_element_type=jnp.float32)
    attn_post, attn_post_back = jax.vjp(norm_gain, attn_lin, gain_attn_out)
    middle = x_flat + attn_post
    ffw_in, ffw_in_back = jax.vjp(norm_gain, middle, gain_ffw_in)
    ffw_in_b = ffw_in.astype(jnp.bfloat16)
    gate_lin = jnp.dot(ffw_in_b, gate_full, preferred_element_type=jnp.float32)
    up_lin = jnp.dot(ffw_in_b, up_full, preferred_element_type=jnp.float32)
    hidden, hidden_back = jax.vjp(gelu_mix, gate_lin, up_lin)
    hidden_b = hidden.astype(jnp.bfloat16)
    ffw_out = jnp.dot(hidden_b, down_full, preferred_element_type=jnp.float32)
    ffw_post, ffw_post_back = jax.vjp(norm_gain, ffw_out, gain_ffw_out)
    outputs = (middle + ffw_post).astype(jnp.bfloat16).reshape(seq_count, row_count, model_width)
    grad_top = cotangent.astype(jnp.float32).reshape(flat_rows, model_width)
    d_ffw_out, grad_ffw_out_gain = ffw_post_back(grad_top)
    d_ffw_out_b = d_ffw_out.astype(jnp.bfloat16)
    grad_down = jnp.einsum("rf,rd->fd", hidden_b, d_ffw_out_b, preferred_element_type=jnp.float32)
    d_hidden = jnp.einsum("rd,fd->rf", d_ffw_out_b, down_full, preferred_element_type=jnp.float32)
    d_gate, d_up = hidden_back(d_hidden)
    d_gate_b = d_gate.astype(jnp.bfloat16)
    d_up_b = d_up.astype(jnp.bfloat16)
    grad_gate = jnp.einsum("rd,rf->df", ffw_in_b, d_gate_b, preferred_element_type=jnp.float32)
    grad_up = jnp.einsum("rd,rf->df", ffw_in_b, d_up_b, preferred_element_type=jnp.float32)
    d_ffw_in = jnp.einsum(
        "rf,df->rd", d_gate_b, gate_full, preferred_element_type=jnp.float32
    ) + jnp.einsum("rf,df->rd", d_up_b, up_full, preferred_element_type=jnp.float32)
    d_middle_part, grad_ffw_in_gain = ffw_in_back(d_ffw_in)
    d_middle = grad_top + d_middle_part
    d_attn_lin, grad_attn_out_gain = attn_post_back(d_middle)
    d_attn_b = d_attn_lin.astype(jnp.bfloat16)
    grad_projection = jnp.einsum(
        "ro,rd->od", attended_b, d_attn_b, preferred_element_type=jnp.float32
    )
    d_attended_b = (
        jnp.einsum("rd,od->ro", d_attn_b, out_full, preferred_element_type=jnp.float32)
        .astype(jnp.bfloat16)
        .reshape(seq_count, row_count, head_count, head_dim)
    )
    d_attended = d_attended_b.astype(jnp.float32)
    row_delta = jnp.einsum("sqhd,shqd->shq", d_attended, attended, precision=lax.Precision.HIGHEST)

    def key_grads(key_piece, value_piece, key_begin):
        mask_now = allowed(key_begin, key_piece.shape[1])
        probabilities = jnp.where(
            mask_now, jnp.exp(raw_scores(key_piece) - log_total[..., None]), 0.0
        )
        d_probs = jnp.einsum(
            "sqhd,skd->shqk", d_attended_b, value_piece, preferred_element_type=jnp.float32
        )
        d_scores = (probabilities * (d_probs - row_delta[..., None])).astype(jnp.bfloat16)
        d_query = (
            jnp.einsum("shqk,skd->sqhd", d_scores, key_piece, preferred_element_type=jnp.float32)
            * att_scale
        )
        d_key = (
            jnp.einsum("shqk,sqhd->skd", d_scores, query_b, preferred_element_type=jnp.float32)
            * att_scale
        )
        d_value = jnp.einsum(
            "shqk,sqhd->skd",
            probabilities.astype(jnp.bfloat16),
            d_attended_b,
            preferred_element_type=jnp.float32,
        )
        return (d_query, jnp.concatenate([d_key, d_value], axis=-1))

    key_back_all, value_back_all = (
        lax.all_gather(key_b, "ctx", axis=1, tiled=True),
        lax.all_gather(value_b, "ctx", axis=1, tiled=True),
    )

    def slice_keys(key_begin, key_count):
        return (
            lax.dynamic_slice_in_dim(key_back_all, key_begin, key_count, 1),
            lax.dynamic_slice_in_dim(value_back_all, key_begin, key_count, 1),
        )

    query_zero = jnp.zeros((seq_count, row_count, head_count, head_dim), jnp.float32)

    def joint_step(block_id, state):
        d_query_sum, key_buffer = state
        key_begin = block_id * key_span
        key_piece, value_piece = slice_keys(key_begin, key_span)
        d_query, d_keyval = key_grads(key_piece, value_piece, key_begin)
        return (
            d_query_sum + d_query,
            lax.dynamic_update_slice_in_dim(key_buffer, d_keyval, key_begin, 1),
        )

    d_query_rot, key_buffer = lax.fori_loop(
        0,
        seq_len // key_span,
        joint_step,
        (query_zero, jnp.zeros((seq_count, seq_len, 2 * head_dim), jnp.float32)),
    )
    d_keyval_own = lax.psum_scatter(key_buffer, "ctx", scatter_dimension=1, tiled=True)
    d_key_rot = d_keyval_own[..., :head_dim]
    d_value = d_keyval_own[..., head_dim:]
    d_query_lin, grad_query_gain = query_side_back(d_query_rot)
    d_key_lin, grad_key_gain = key_side_back(d_key_rot)
    d_query_b = d_query_lin.astype(jnp.bfloat16)
    d_key_b = d_key_lin.astype(jnp.bfloat16)
    d_value_b = d_value.reshape(flat_rows, head_dim).astype(jnp.bfloat16)
    grad_query = jnp.einsum("rd,rq->dq", attn_in_b, d_query_b, preferred_element_type=jnp.float32)
    grad_key = jnp.einsum("rd,rq->dq", attn_in_b, d_key_b, preferred_element_type=jnp.float32)
    grad_value = jnp.einsum("rd,rq->dq", attn_in_b, d_value_b, preferred_element_type=jnp.float32)
    d_attn_in = jnp.einsum("rq,dq->rd", d_query_b, query_full, preferred_element_type=jnp.float32)
    d_attn_in = d_attn_in + jnp.einsum(
        "rq,dq->rd", d_key_b, key_full, preferred_element_type=jnp.float32
    )
    d_attn_in = d_attn_in + jnp.einsum(
        "rq,dq->rd", d_value_b, value_full, preferred_element_type=jnp.float32
    )
    d_input_part, grad_attn_in_gain = attn_in_back(d_attn_in)
    input_grad = (
        (d_middle + d_input_part).astype(jnp.bfloat16).reshape(seq_count, row_count, model_width)
    )
    if fast:
        gain_rows = [
            grad_attn_in_gain,
            grad_attn_out_gain,
            grad_ffw_in_gain,
            grad_ffw_out_gain,
            jnp.pad(grad_query_gain, (0, model_width - head_dim)),
            jnp.pad(grad_key_gain, (0, model_width - head_dim)),
        ]
        gain_pack = jnp.pad(jnp.stack(gain_rows), ((0, 2), (0, 0)))
        grads_in = jnp.concatenate([grad_query, grad_key, grad_value], axis=1)
        t_down, t_gate, t_up, t_projection, t_in, gain_totals = reduce_all(
            [
                grad_down.astype(jnp.bfloat16),
                grad_gate.astype(jnp.bfloat16),
                grad_up.astype(jnp.bfloat16),
                grad_projection.astype(jnp.bfloat16),
                grads_in.astype(jnp.bfloat16),
            ],
            (False, True, True, False, True),
            gain_pack,
        )
        part = lax.axis_index("fsdp")
        wide = head_count * head_dim
        results = [
            t_in[:, :wide],
            t_in[:, wide : wide + head_dim],
            t_in[:, wide + head_dim :],
            t_projection,
            t_gate,
            t_up,
            t_down,
        ]
        results = [item.astype(jnp.float32) for item in results]
        for at in range(6):
            size = (model_width if at < 4 else head_dim) // 4
            results.append(lax.dynamic_slice_in_dim(gain_totals[at], part * size, size, 0))
        return (outputs, input_grad) + tuple(results)
    shards = (
        lax.psum_scatter(
            grad_query.astype(jnp.bfloat16), "fsdp", scatter_dimension=0, tiled=True
        ).astype(jnp.float32),
        lax.psum_scatter(
            grad_key.astype(jnp.bfloat16), "fsdp", scatter_dimension=0, tiled=True
        ).astype(jnp.float32),
        lax.psum_scatter(
            grad_value.astype(jnp.bfloat16), "fsdp", scatter_dimension=0, tiled=True
        ).astype(jnp.float32),
        lax.psum_scatter(
            grad_projection.astype(jnp.bfloat16), "fsdp", scatter_dimension=0, tiled=True
        ).astype(jnp.float32),
        lax.psum_scatter(
            grad_gate.astype(jnp.bfloat16), "fsdp", scatter_dimension=0, tiled=True
        ).astype(jnp.float32),
        lax.psum_scatter(
            grad_up.astype(jnp.bfloat16), "fsdp", scatter_dimension=0, tiled=True
        ).astype(jnp.float32),
        lax.psum_scatter(
            grad_down.astype(jnp.bfloat16), "fsdp", scatter_dimension=0, tiled=True
        ).astype(jnp.float32),
        lax.psum_scatter(
            grad_attn_in_gain.astype(jnp.bfloat16), "fsdp", scatter_dimension=0, tiled=True
        ).astype(jnp.float32),
        lax.psum_scatter(
            grad_attn_out_gain.astype(jnp.bfloat16), "fsdp", scatter_dimension=0, tiled=True
        ).astype(jnp.float32),
        lax.psum_scatter(
            grad_ffw_in_gain.astype(jnp.bfloat16), "fsdp", scatter_dimension=0, tiled=True
        ).astype(jnp.float32),
        lax.psum_scatter(
            grad_ffw_out_gain.astype(jnp.bfloat16), "fsdp", scatter_dimension=0, tiled=True
        ).astype(jnp.float32),
        lax.psum_scatter(
            grad_query_gain.astype(jnp.bfloat16), "fsdp", scatter_dimension=0, tiled=True
        ).astype(jnp.float32),
        lax.psum_scatter(
            grad_key_gain.astype(jnp.bfloat16), "fsdp", scatter_dimension=0, tiled=True
        ).astype(jnp.float32),
    )
    totals = lax.psum(
        (
            shards[0],
            shards[1],
            shards[2],
            shards[3],
            shards[4],
            shards[5],
            shards[6],
            shards[7],
            shards[8],
            shards[9],
            shards[10],
            shards[11],
            shards[12],
        ),
        "ctx",
    )
    return (outputs, input_grad) + tuple(totals)


def solution(mesh):
    in_specs = (
        P("fsdp", "ctx", None),
        P("fsdp", "ctx", None),
        P("fsdp"),
        P("fsdp", None),
        P("fsdp", None),
        P("fsdp", None),
        P("fsdp", None),
        P("fsdp", None),
        P("fsdp", None),
        P("fsdp", None),
        P("fsdp"),
        P("fsdp"),
        P("fsdp"),
        P("fsdp"),
        P("fsdp"),
        P("fsdp"),
    )
    out_specs = (
        P("fsdp", "ctx", None),
        P("fsdp", "ctx", None),
        P("fsdp", None),
        P("fsdp", None),
        P("fsdp", None),
        P("fsdp", None),
        P("fsdp", None),
        P("fsdp", None),
        P("fsdp", None),
        P("fsdp"),
        P("fsdp"),
        P("fsdp"),
        P("fsdp"),
        P("fsdp"),
        P("fsdp"),
    )
    return jax.shard_map(body, mesh=mesh, in_specs=in_specs, out_specs=out_specs, check_vma=False)
```

```python
import math

import jax
import jax.numpy as jnp
from jax import lax
from jax.experimental import pallas as pl
from jax.experimental.pallas import tpu as pltpu
from jax.sharding import PartitionSpec as P

EPSILON = 1e-06
MASKED_SCORE = -1e30
ROPE_BASE = 1000000.0


def norm_gain(values, gain_vec):
    return (
        values
        * lax.rsqrt(jnp.mean(values * values, axis=-1, keepdims=True) + EPSILON)
        * (1.0 + gain_vec)
    )


def rotate(values, positions):
    half_dim = values.shape[-1] // 2
    inverse = ROPE_BASE ** (-(jnp.arange(half_dim).astype(jnp.float32) * 2.0) / values.shape[-1])
    angles = positions.astype(jnp.float32)[:, None] * inverse[None, :]
    cosine = jnp.cos(angles)[:, None, :]
    sine_part = jnp.sin(angles)[:, None, :]
    first_half = values[..., :half_dim]
    second_half = values[..., half_dim:]
    return jnp.concatenate(
        [
            first_half * cosine - second_half * sine_part,
            second_half * cosine + first_half * sine_part,
        ],
        axis=-1,
    )


MESH_ID = pl.DeviceIdType.MESH
VMEM_BYTES = 56 * 1024 * 1024


def place():
    ctx = lax.axis_index("ctx")
    fsdp = lax.axis_index("fsdp")
    return lax.rem(ctx, 2), lax.div(ctx, 2), lax.rem(fsdp, 2), lax.div(fsdp, 2)


def device(y, z, core, x):
    return (z * 2 + y, x * 2 + core)


def greet(peers):
    barrier = pltpu.get_barrier_semaphore()
    for peer in peers:
        pl.semaphore_signal(barrier, inc=1, device_id=peer, device_id_type=MESH_ID)
    pl.semaphore_wait(barrier, len(peers))


def reduce_kernel(by_columns, *refs):
    count = len(by_columns)
    grads, gains = refs[:count], refs[count]
    outs, gain_out = refs[count + 1 : 2 * count + 1], refs[2 * count + 1]
    refs = refs[2 * count + 2 :]
    core_in, x_in, y_in, z_in = (refs[i * count : (i + 1) * count] for i in range(4))
    gain_in, gain_sum, send_sem, recv_sem, gain_send, gain_recv = refs[4 * count :]
    y, z, core, x = place()
    core_peer = device(y, z, 1 - core, x)
    x_peer = device(y, z, core, 1 - x)
    y_peer = device(1 - y, z, core, x)
    z_at = [lax.rem(z + hop, 4) for hop in (1, 2, 3)]
    z_peers = [device(y, other, core, x) for other in z_at]
    greet([core_peer, x_peer, y_peer] + z_peers)

    def quarter(item, ref, at):
        if by_columns[item]:
            width = ref.shape[1] // 4
            return ref.at[:, pl.ds(pl.multiple_of(at * width, 128), width)]
        width = ref.shape[0] // 4
        return ref.at[pl.ds(pl.multiple_of(at * width, 16), width), :]

    def copy(item, slot, source, target, peer):
        return pltpu.make_async_remote_copy(
            src_ref=source,
            dst_ref=target,
            send_sem=send_sem.at[item, slot],
            recv_sem=recv_sem.at[item, slot],
            device_id=peer,
            device_id_type=MESH_ID,
        )

    def gain_copy(slot, source, peer):
        return pltpu.make_async_remote_copy(
            src_ref=source,
            dst_ref=gain_in.at[slot],
            send_sem=gain_send.at[slot],
            recv_sem=gain_recv.at[slot],
            device_id=peer,
            device_id_type=MESH_ID,
        )

    def add_rows(target, others):
        rows = target.shape[0]

        @pl.loop(0, rows // 16)
        def _(step):
            span = pl.ds(pl.multiple_of(step * 16, 16), 16)
            total = others[0][span, :].astype(jnp.float32)
            for other in others[1:]:
                total = total + other[span, :].astype(jnp.float32)
            target[span, :] = total.astype(target.dtype)

    copies = [[None] * 10 for _ in range(count)]
    gain_copies = [None] * 6

    def stage_core(item):
        copies[item][0] = copy(item, 0, grads[item].at[:, 1 - core], core_in[item], core_peer)
        copies[item][0].start()

    def stage_x(item):
        copies[item][0].wait_recv()
        for side in range(2):
            for half in range(2):
                target = core_in[item].at[side, half]
                add_rows(target, [target, grads[item].at[side, core, half]])
        copies[item][1] = copy(item, 1, core_in[item].at[1 - x], x_in[item], x_peer)
        copies[item][1].start()

    def stage_y(item):
        copies[item][1].wait_recv()
        for half in range(2):
            target = x_in[item].at[half]
            add_rows(target, [target, core_in[item].at[x, half]])
        copies[item][2] = copy(item, 2, x_in[item].at[1 - y], y_in[item], y_peer)
        copies[item][2].start()

    def stage_z(item):
        copies[item][2].wait_recv()
        add_rows(y_in[item], [y_in[item], x_in[item].at[y]])
        for hop in range(3):
            copies[item][3 + hop] = copy(
                item, 3 + hop, quarter(item, y_in[item], z_at[hop]), z_in[item].at[hop], z_peers[hop]
            )
            copies[item][3 + hop].start()

    def stage_back_z(item):
        for hop in range(3):
            copies[item][3 + hop].wait_recv()
        mine = quarter(item, outs[item].at[y], z)
        add_rows(mine, [quarter(item, y_in[item], z)] + [z_in[item].at[hop] for hop in range(3)])
        for hop in range(3):
            copies[item][6 + hop] = copy(item, 6 + hop, mine, mine, z_peers[hop])
            copies[item][6 + hop].start()

    def stage_back_y(item):
        for hop in range(3):
            copies[item][6 + hop].wait_recv()
        copies[item][9] = copy(item, 9, outs[item].at[y], outs[item].at[y], y_peer)
        copies[item][9].start()

    def gain_step(step):
        if step == 0:
            gain_copies[0] = gain_copy(0, gains, core_peer)
            gain_copies[0].start()
        elif step <= 2:
            gain_copies[step - 1].wait_recv()
            before = gains if step == 1 else gain_sum.at[step - 2]
            gain_sum[step - 1] = before[...] + gain_in[step - 1]
            gain_copies[step] = gain_copy(step, gain_sum.at[step - 1], (x_peer, y_peer)[step - 1])
            gain_copies[step].start()
        elif step == 3:
            gain_copies[2].wait_recv()
            gain_sum[2] = gain_sum[1] + gain_in[2]
            for hop in range(3):
                gain_copies[3 + hop] = gain_copy(3 + hop, gain_sum.at[2], z_peers[hop])
                gain_copies[3 + hop].start()
        elif step == 4:
            for hop in range(3):
                gain_copies[3 + hop].wait_recv()
            gain_out[...] = (gain_sum[2] + gain_in[4]) + (gain_in[3] + gain_in[5])

    for item in range(count):
        stage_core(item)
    stages = (stage_x, stage_y, stage_z, stage_back_z, stage_back_y)
    for tick in range(count + len(stages) - 1):
        for at, stage in enumerate(stages):
            if 0 <= tick - at < count:
                stage(tick - at)
        gain_step(tick)
    for item in range(count):
        copies[item][9].wait_recv()
    for item in range(count):
        for slot in range(10):
            copies[item][slot].wait_send()
    for slot in range(6):
        gain_copies[slot].wait_send()


def reduce_all(grads, by_columns, gains):
    shaped, outs, scratch = [], [], [[], [], [], []]
    for grad, columns_split in zip(grads, by_columns):
        rows, columns = grad.shape[0] // 8, grad.shape[1]
        shaped.append(grad.reshape(2, 2, 2, rows, columns))
        outs.append(jax.ShapeDtypeStruct((2, rows, columns), jnp.bfloat16))
        piece = (rows, columns // 4) if columns_split else (rows // 4, columns)
        scratch[0].append(pltpu.VMEM((2, 2, rows, columns), jnp.bfloat16))
        scratch[1].append(pltpu.VMEM((2, rows, columns), jnp.bfloat16))
        scratch[2].append(pltpu.VMEM((rows, columns), jnp.bfloat16))
        scratch[3].append(pltpu.VMEM((3,) + piece, jnp.bfloat16))
    count = len(grads)
    outs.append(jax.ShapeDtypeStruct(gains.shape, jnp.float32))
    sent = sum(grad.size for grad in grads)

    def kernel(*refs):
        reduce_kernel(by_columns, *refs)

    results = pl.pallas_call(
        kernel,
        out_shape=outs,
        in_specs=[pl.BlockSpec(memory_space=pltpu.VMEM)] * (count + 1),
        out_specs=[pl.BlockSpec(memory_space=pltpu.VMEM)] * (count + 1),
        scratch_shapes=scratch[0]
        + scratch[1]
        + scratch[2]
        + scratch[3]
        + [
            pltpu.VMEM((6,) + gains.shape, jnp.float32),
            pltpu.VMEM((3,) + gains.shape, jnp.float32),
            pltpu.SemaphoreType.DMA((count, 10)),
            pltpu.SemaphoreType.DMA((count, 10)),
            pltpu.SemaphoreType.DMA((6,)),
            pltpu.SemaphoreType.DMA((6,)),
        ],
        compiler_params=pltpu.CompilerParams(
            collective_id=1, has_side_effects=True, vmem_limit_bytes=VMEM_BYTES
        ),
        cost_estimate=pl.CostEstimate(flops=2 * sent, bytes_accessed=4 * sent, transcendentals=0),
        name="reduce_grads",
    )(*shaped, gains)
    return [
        result.reshape(2 * result.shape[1], result.shape[2]) for result in results[:-1]
    ] + [results[-1]]


def gather_kernel(count, *refs):
    shards, outs = refs[:count], refs[count : 2 * count]
    send_sem, recv_sem, own_sem = refs[2 * count :]
    y, z, core, x = place()
    core_peer = device(y, z, 1 - core, x)
    x_peer = device(y, z, core, 1 - x)
    y_peer = device(1 - y, z, core, x)
    greet([core_peer, x_peer, y_peer])

    def send(item, slot, source, target, peer):
        copy = pltpu.make_async_remote_copy(
            src_ref=source,
            dst_ref=target,
            send_sem=send_sem.at[item, slot],
            recv_sem=recv_sem.at[item, slot],
            device_id=peer,
            device_id_type=MESH_ID,
        )
        copy.start()
        return copy

    copies = [[None] * 5 for _ in range(count)]
    for item in range(count):
        copies[item][1] = send(item, 1, shards[item].at[y], outs[item].at[x, core, y], x_peer)
    for item in range(count):
        copies[item][0] = send(item, 0, shards[item], outs[item].at[x, core], core_peer)
    own = [
        pltpu.make_async_copy(shards[item], outs[item].at[x, core], own_sem.at[item])
        for item in range(count)
    ]
    for copy in own:
        copy.start()
    for tick in range(count + 1):
        if tick < count:
            copies[tick][1].wait_recv()
            here = outs[tick].at[1 - x, core, y]
            copies[tick][2] = send(tick, 2, here, here, y_peer)
            copies[tick][3] = send(tick, 3, here, here, core_peer)
        if tick >= 1:
            copies[tick - 1][2].wait_recv()
            there = outs[tick - 1].at[1 - x, core, 1 - y]
            copies[tick - 1][4] = send(tick - 1, 4, there, there, core_peer)
    for item in range(count):
        own[item].wait()
        for slot in (0, 3, 4):
            copies[item][slot].wait_recv()
        for slot in range(5):
            copies[item][slot].wait_send()


def gather_all(shards):
    shaped = [item.reshape(2, item.shape[0] // 2, item.shape[1]) for item in shards]
    count = len(shards)
    sent = sum(item.size for item in shards)

    def kernel(*refs):
        gather_kernel(count, *refs)

    results = pl.pallas_call(
        kernel,
        out_shape=[jax.ShapeDtypeStruct((2, 2) + item.shape, item.dtype) for item in shaped],
        in_specs=[pl.BlockSpec(memory_space=pltpu.VMEM)] * count,
        out_specs=[pl.BlockSpec(memory_space=pltpu.VMEM)] * count,
        scratch_shapes=[
            pltpu.SemaphoreType.DMA((count, 5)),
            pltpu.SemaphoreType.DMA((count, 5)),
            pltpu.SemaphoreType.DMA((count,)),
        ],
        compiler_params=pltpu.CompilerParams(
            collective_id=2, has_side_effects=True, vmem_limit_bytes=VMEM_BYTES
        ),
        cost_estimate=pl.CostEstimate(flops=0, bytes_accessed=10 * sent, transcendentals=0),
        name="gather_weights",
    )(*shaped)
    return [
        result.reshape(4 * item.shape[0], item.shape[1]) for result, item in zip(results, shards)
    ]


def gather_fast(weights, gains):
    query, key, value, out, gate, up, down = weights
    wide = 256
    rows = [jnp.pad(gain, (0, wide - gain.shape[0])) for gain in gains]
    pack = jnp.pad(jnp.stack(rows), ((0, 16 - len(rows)), (0, 0)))
    joined, out, gate, up, down, packs = gather_all(
        [
            jnp.concatenate([query, key, value], axis=1),
            out,
            gate,
            up,
            down,
            jnp.concatenate([pack, pack], axis=0),
        ]
    )
    first, second = query.shape[1], query.shape[1] + key.shape[1]
    packs = packs.reshape(4, 2, 16, wide)
    whole_gains = [
        packs[:, 0, at, : gain.shape[0]].reshape(4 * gain.shape[0]) for at, gain in enumerate(gains)
    ]
    return (
        joined[:, :first],
        joined[:, first:second],
        joined[:, second:],
        out,
        gate,
        up,
        down,
        *whole_gains,
    )


def gelu_mix(gate_in, up_in):
    return jax.nn.gelu(gate_in, approximate=True) * up_in


def body(
    inputs,
    cotangent,
    lengths,
    query_weight,
    key_weight,
    value_weight,
    out_weight,
    gate_weight,
    up_weight,
    down_weight,
    pre_attn_gain,
    post_attn_gain,
    pre_ffw_gain,
    post_ffw_gain,
    query_gain,
    key_gain,
):
    seq_count, row_count, model_width = inputs.shape
    fast = lax.axis_size("ctx") == 8 and lax.axis_size("fsdp") == 4
    weights = (
        query_weight,
        key_weight,
        value_weight,
        out_weight,
        gate_weight,
        up_weight,
        down_weight,
    )
    gains = (
        pre_attn_gain,
        post_attn_gain,
        pre_ffw_gain,
        post_ffw_gain,
        query_gain,
        key_gain,
    )
    if fast:
        gathered = gather_fast(weights, gains)
    else:
        gathered = tuple(
            lax.all_gather(item, "fsdp", axis=0, tiled=True) for item in weights + gains
        )
    (
        query_full,
        key_full,
        value_full,
        out_full,
        gate_full,
        up_full,
        down_full,
        gain_attn_in,
        gain_attn_out,
        gain_ffw_in,
        gain_ffw_out,
        gain_query,
        gain_key,
    ) = gathered
    gain_attn_in = gain_attn_in.astype(jnp.float32)
    gain_attn_out = gain_attn_out.astype(jnp.float32)
    gain_ffw_in = gain_ffw_in.astype(jnp.float32)
    gain_ffw_out = gain_ffw_out.astype(jnp.float32)
    gain_query = gain_query.astype(jnp.float32)
    gain_key = gain_key.astype(jnp.float32)
    head_dim = key_full.shape[1]
    head_count = query_full.shape[1] // head_dim
    seq_len = row_count * lax.axis_size("ctx")
    key_span = math.gcd(512, seq_len)
    att_scale = head_dim ** (-0.5)
    flat_rows = seq_count * row_count
    positions = lax.axis_index("ctx") * row_count + jnp.arange(row_count, dtype=jnp.int32)
    x_flat = inputs.astype(jnp.float32).reshape(flat_rows, model_width)
    attn_in, attn_in_back = jax.vjp(norm_gain, x_flat, gain_attn_in)
    attn_in_b = attn_in.astype(jnp.bfloat16)
    query_lin = jnp.dot(attn_in_b, query_full, preferred_element_type=jnp.float32)
    key_lin = jnp.dot(attn_in_b, key_full, preferred_element_type=jnp.float32)
    value_lin = jnp.dot(attn_in_b, value_full, preferred_element_type=jnp.float32)

    def query_side(lin_values, gain_vec):
        return rotate(
            norm_gain(lin_values.reshape(seq_count, row_count, head_count, head_dim), gain_vec),
            positions,
        )

    def key_side(lin_values, gain_vec):
        return rotate(
            norm_gain(lin_values.reshape(seq_count, row_count, 1, head_dim), gain_vec), positions
        )[:, :, 0, :]

    query_rot, query_side_back = jax.vjp(query_side, query_lin, gain_query)
    key_rot, key_side_back = jax.vjp(key_side, key_lin, gain_key)
    query_b = query_rot.astype(jnp.bfloat16)
    key_b = key_rot.astype(jnp.bfloat16)
    value_b = value_lin.reshape(seq_count, row_count, head_dim).astype(jnp.bfloat16)

    def allowed(key_begin, key_count):
        key_pos = key_begin + jnp.arange(key_count, dtype=jnp.int32)
        causal = key_pos[None, :] <= positions[:, None]
        live = key_pos[None, :] < lengths[:, None]
        return (causal[None] & live[:, None, :])[:, None]

    def raw_scores(key_piece):
        return (
            jnp.einsum("sqhd,skd->shqk", query_b, key_piece, preferred_element_type=jnp.float32)
            * att_scale
        )

    stat_shape = (seq_count, head_count, row_count)
    running_max = jnp.full(stat_shape, MASKED_SCORE, jnp.float32)
    key_piece = lax.all_gather(key_b, "ctx", axis=1, tiled=True)
    value_piece = lax.all_gather(value_b, "ctx", axis=1, tiled=True)
    mask_now = allowed(jnp.int32(0), key_piece.shape[1])
    scores = jnp.where(mask_now, raw_scores(key_piece), MASKED_SCORE)
    new_max = jnp.maximum(running_max, jnp.max(scores, axis=-1))
    weights = jnp.where(mask_now, jnp.exp(scores - new_max[..., None]), 0.0)
    new_sum = jnp.sum(weights, axis=-1)
    new_acc = jnp.einsum(
        "shqk,skd->shqd",
        weights.astype(jnp.bfloat16),
        value_piece,
        preferred_element_type=jnp.float32,
    )
    final_state = (new_max, new_sum, new_acc)
    final_max, final_sum, final_acc = final_state
    attended = final_acc / final_sum[..., None]
    log_total = final_max + jnp.log(final_sum)
    attended_b = (
        attended.transpose(0, 2, 1, 3)
        .reshape(flat_rows, head_count * head_dim)
        .astype(jnp.bfloat16)
    )
    attn_lin = jnp.dot(attended_b, out_full, preferred_element_type=jnp.float32)
    attn_post, attn_post_back = jax.vjp(norm_gain, attn_lin, gain_attn_out)
    middle = x_flat + attn_post
    ffw_in, ffw_in_back = jax.vjp(norm_gain, middle, gain_ffw_in)
    ffw_in_b = ffw_in.astype(jnp.bfloat16)
    gate_lin = jnp.dot(ffw_in_b, gate_full, preferred_element_type=jnp.float32)
    up_lin = jnp.dot(ffw_in_b, up_full, preferred_element_type=jnp.float32)
    hidden, hidden_back = jax.vjp(gelu_mix, gate_lin, up_lin)
    hidden_b = hidden.astype(jnp.bfloat16)
    ffw_out = jnp.dot(hidden_b, down_full, preferred_element_type=jnp.float32)
    ffw_post, ffw_post_back = jax.vjp(norm_gain, ffw_out, gain_ffw_out)
    outputs = (middle + ffw_post).astype(jnp.bfloat16).reshape(seq_count, row_count, model_width)
    grad_top = cotangent.astype(jnp.float32).reshape(flat_rows, model_width)
    d_ffw_out, grad_ffw_out_gain = ffw_post_back(grad_top)
    d_ffw_out_b = d_ffw_out.astype(jnp.bfloat16)
    grad_down = jnp.einsum("rf,rd->fd", hidden_b, d_ffw_out_b, preferred_element_type=jnp.float32)
    d_hidden = jnp.einsum("rd,fd->rf", d_ffw_out_b, down_full, preferred_element_type=jnp.float32)
    d_gate, d_up = hidden_back(d_hidden)
    d_gate_b = d_gate.astype(jnp.bfloat16)
    d_up_b = d_up.astype(jnp.bfloat16)
    grad_gate = jnp.einsum("rd,rf->df", ffw_in_b, d_gate_b, preferred_element_type=jnp.float32)
    grad_up = jnp.einsum("rd,rf->df", ffw_in_b, d_up_b, preferred_element_type=jnp.float32)
    d_ffw_in = jnp.einsum(
        "rf,df->rd", d_gate_b, gate_full, preferred_element_type=jnp.float32
    ) + jnp.einsum("rf,df->rd", d_up_b, up_full, preferred_element_type=jnp.float32)
    d_middle_part, grad_ffw_in_gain = ffw_in_back(d_ffw_in)
    d_middle = grad_top + d_middle_part
    d_attn_lin, grad_attn_out_gain = attn_post_back(d_middle)
    d_attn_b = d_attn_lin.astype(jnp.bfloat16)
    grad_projection = jnp.einsum(
        "ro,rd->od", attended_b, d_attn_b, preferred_element_type=jnp.float32
    )
    d_attended_b = (
        jnp.einsum("rd,od->ro", d_attn_b, out_full, preferred_element_type=jnp.float32)
        .astype(jnp.bfloat16)
        .reshape(seq_count, row_count, head_count, head_dim)
    )
    d_attended = d_attended_b.astype(jnp.float32)
    row_delta = jnp.einsum("sqhd,shqd->shq", d_attended, attended, precision=lax.Precision.HIGHEST)

    def key_grads(key_piece, value_piece, key_begin):
        mask_now = allowed(key_begin, key_piece.shape[1])
        probabilities = jnp.where(
            mask_now, jnp.exp(raw_scores(key_piece) - log_total[..., None]), 0.0
        )
        d_probs = jnp.einsum(
            "sqhd,skd->shqk", d_attended_b, value_piece, preferred_element_type=jnp.float32
        )
        d_scores = (probabilities * (d_probs - row_delta[..., None])).astype(jnp.bfloat16)
        d_query = (
            jnp.einsum("shqk,skd->sqhd", d_scores, key_piece, preferred_element_type=jnp.float32)
            * att_scale
        )
        d_key = (
            jnp.einsum("shqk,sqhd->skd", d_scores, query_b, preferred_element_type=jnp.float32)
            * att_scale
        )
        d_value = jnp.einsum(
            "shqk,sqhd->skd",
            probabilities.astype(jnp.bfloat16),
            d_attended_b,
            preferred_element_type=jnp.float32,
        )
        return (d_query, jnp.concatenate([d_key, d_value], axis=-1))

    key_back_all, value_back_all = (
        lax.all_gather(key_b, "ctx", axis=1, tiled=True),
        lax.all_gather(value_b, "ctx", axis=1, tiled=True),
    )

    def slice_keys(key_begin, key_count):
        return (
            lax.dynamic_slice_in_dim(key_back_all, key_begin, key_count, 1),
            lax.dynamic_slice_in_dim(value_back_all, key_begin, key_count, 1),
        )

    query_zero = jnp.zeros((seq_count, row_count, head_count, head_dim), jnp.float32)

    def joint_step(block_id, state):
        d_query_sum, key_buffer = state
        key_begin = block_id * key_span
        key_piece, value_piece = slice_keys(key_begin, key_span)
        d_query, d_keyval = key_grads(key_piece, value_piece, key_begin)
        return (
            d_query_sum + d_query,
            lax.dynamic_update_slice_in_dim(key_buffer, d_keyval, key_begin, 1),
        )

    if seq_len <= 1024:
        d_query_rot, key_buffer = key_grads(key_back_all, value_back_all, jnp.int32(0))
    else:
        d_query_rot, key_buffer = lax.fori_loop(
            0,
            seq_len // key_span,
            joint_step,
            (query_zero, jnp.zeros((seq_count, seq_len, 2 * head_dim), jnp.float32)),
        )
    d_keyval_own = lax.psum_scatter(
        key_buffer.astype(jnp.bfloat16), "ctx", scatter_dimension=1, tiled=True
    ).astype(jnp.float32)
    d_key_rot = d_keyval_own[..., :head_dim]
    d_value = d_keyval_own[..., head_dim:]
    d_query_lin, grad_query_gain = query_side_back(d_query_rot)
    d_key_lin, grad_key_gain = key_side_back(d_key_rot)
    d_query_b = d_query_lin.astype(jnp.bfloat16)
    d_key_b = d_key_lin.astype(jnp.bfloat16)
    d_value_b = d_value.reshape(flat_rows, head_dim).astype(jnp.bfloat16)
    grad_query = jnp.einsum("rd,rq->dq", attn_in_b, d_query_b, preferred_element_type=jnp.float32)
    grad_key = jnp.einsum("rd,rq->dq", attn_in_b, d_key_b, preferred_element_type=jnp.float32)
    grad_value = jnp.einsum("rd,rq->dq", attn_in_b, d_value_b, preferred_element_type=jnp.float32)
    d_attn_in = jnp.einsum("rq,dq->rd", d_query_b, query_full, preferred_element_type=jnp.float32)
    d_attn_in = d_attn_in + jnp.einsum(
        "rq,dq->rd", d_key_b, key_full, preferred_element_type=jnp.float32
    )
    d_attn_in = d_attn_in + jnp.einsum(
        "rq,dq->rd", d_value_b, value_full, preferred_element_type=jnp.float32
    )
    d_input_part, grad_attn_in_gain = attn_in_back(d_attn_in)
    input_grad = (
        (d_middle + d_input_part).astype(jnp.bfloat16).reshape(seq_count, row_count, model_width)
    )
    if fast:
        gain_rows = [
            grad_attn_in_gain,
            grad_attn_out_gain,
            grad_ffw_in_gain,
            grad_ffw_out_gain,
            jnp.pad(grad_query_gain, (0, model_width - head_dim)),
            jnp.pad(grad_key_gain, (0, model_width - head_dim)),
        ]
        gain_pack = jnp.pad(jnp.stack(gain_rows), ((0, 2), (0, 0)))
        grads_in = jnp.concatenate([grad_query, grad_key, grad_value], axis=1)
        t_down, t_gate, t_up, t_projection, t_in, gain_totals = reduce_all(
            [
                grad_down.astype(jnp.bfloat16),
                grad_gate.astype(jnp.bfloat16),
                grad_up.astype(jnp.bfloat16),
                grad_projection.astype(jnp.bfloat16),
                grads_in.astype(jnp.bfloat16),
            ],
            (False, True, True, False, True),
            gain_pack,
        )
        part = lax.axis_index("fsdp")
        wide = head_count * head_dim
        results = [
            t_in[:, :wide],
            t_in[:, wide : wide + head_dim],
            t_in[:, wide + head_dim :],
            t_projection,
            t_gate,
            t_up,
            t_down,
        ]
        results = [item.astype(jnp.float32) for item in results]
        for at in range(6):
            size = (model_width if at < 4 else head_dim) // 4
            results.append(lax.dynamic_slice_in_dim(gain_totals[at], part * size, size, 0))
        return (outputs, input_grad) + tuple(results)
    shards = (
        lax.psum_scatter(
            grad_query.astype(jnp.bfloat16), "fsdp", scatter_dimension=0, tiled=True
        ).astype(jnp.float32),
        lax.psum_scatter(
            grad_key.astype(jnp.bfloat16), "fsdp", scatter_dimension=0, tiled=True
        ).astype(jnp.float32),
        lax.psum_scatter(
            grad_value.astype(jnp.bfloat16), "fsdp", scatter_dimension=0, tiled=True
        ).astype(jnp.float32),
        lax.psum_scatter(
            grad_projection.astype(jnp.bfloat16), "fsdp", scatter_dimension=0, tiled=True
        ).astype(jnp.float32),
        lax.psum_scatter(
            grad_gate.astype(jnp.bfloat16), "fsdp", scatter_dimension=0, tiled=True
        ).astype(jnp.float32),
        lax.psum_scatter(
            grad_up.astype(jnp.bfloat16), "fsdp", scatter_dimension=0, tiled=True
        ).astype(jnp.float32),
        lax.psum_scatter(
            grad_down.astype(jnp.bfloat16), "fsdp", scatter_dimension=0, tiled=True
        ).astype(jnp.float32),
        lax.psum_scatter(
            grad_attn_in_gain.astype(jnp.bfloat16), "fsdp", scatter_dimension=0, tiled=True
        ).astype(jnp.float32),
        lax.psum_scatter(
            grad_attn_out_gain.astype(jnp.bfloat16), "fsdp", scatter_dimension=0, tiled=True
        ).astype(jnp.float32),
        lax.psum_scatter(
            grad_ffw_in_gain.astype(jnp.bfloat16), "fsdp", scatter_dimension=0, tiled=True
        ).astype(jnp.float32),
        lax.psum_scatter(
            grad_ffw_out_gain.astype(jnp.bfloat16), "fsdp", scatter_dimension=0, tiled=True
        ).astype(jnp.float32),
        lax.psum_scatter(
            grad_query_gain.astype(jnp.bfloat16), "fsdp", scatter_dimension=0, tiled=True
        ).astype(jnp.float32),
        lax.psum_scatter(
            grad_key_gain.astype(jnp.bfloat16), "fsdp", scatter_dimension=0, tiled=True
        ).astype(jnp.float32),
    )
    totals = lax.psum(
        (
            shards[0],
            shards[1],
            shards[2],
            shards[3],
            shards[4],
            shards[5],
            shards[6],
            shards[7],
            shards[8],
            shards[9],
            shards[10],
            shards[11],
            shards[12],
        ),
        "ctx",
    )
    return (outputs, input_grad) + tuple(totals)


def solution(mesh):
    in_specs = (
        P("fsdp", "ctx", None),
        P("fsdp", "ctx", None),
        P("fsdp"),
        P("fsdp", None),
        P("fsdp", None),
        P("fsdp", None),
        P("fsdp", None),
        P("fsdp", None),
        P("fsdp", None),
        P("fsdp", None),
        P("fsdp"),
        P("fsdp"),
        P("fsdp"),
        P("fsdp"),
        P("fsdp"),
        P("fsdp"),
    )
    out_specs = (
        P("fsdp", "ctx", None),
        P("fsdp", "ctx", None),
        P("fsdp", None),
        P("fsdp", None),
        P("fsdp", None),
        P("fsdp", None),
        P("fsdp", None),
        P("fsdp", None),
        P("fsdp", None),
        P("fsdp"),
        P("fsdp"),
        P("fsdp"),
        P("fsdp"),
        P("fsdp"),
        P("fsdp"),
    )
    return jax.shard_map(body, mesh=mesh, in_specs=in_specs, out_specs=out_specs, check_vma=False)
```

```python
import math

import jax
import jax.numpy as jnp
from jax import lax
from jax.experimental import pallas as pl
from jax.experimental.pallas import tpu as pltpu
from jax.sharding import PartitionSpec as P

EPSILON = 1e-06
MASKED_SCORE = -1e30
ROPE_BASE = 1000000.0


def norm_gain(values, gain_vec):
    return (
        values
        * lax.rsqrt(jnp.mean(values * values, axis=-1, keepdims=True) + EPSILON)
        * (1.0 + gain_vec)
    )


def rotate(values, positions):
    half_dim = values.shape[-1] // 2
    inverse = ROPE_BASE ** (-(jnp.arange(half_dim).astype(jnp.float32) * 2.0) / values.shape[-1])
    angles = positions.astype(jnp.float32)[:, None] * inverse[None, :]
    cosine = jnp.cos(angles)[:, None, :]
    sine_part = jnp.sin(angles)[:, None, :]
    first_half = values[..., :half_dim]
    second_half = values[..., half_dim:]
    return jnp.concatenate(
        [
            first_half * cosine - second_half * sine_part,
            second_half * cosine + first_half * sine_part,
        ],
        axis=-1,
    )


MESH_ID = pl.DeviceIdType.MESH
VMEM_BYTES = 56 * 1024 * 1024


def place():
    ctx = lax.axis_index("ctx")
    fsdp = lax.axis_index("fsdp")
    return lax.rem(ctx, 2), lax.div(ctx, 2), lax.rem(fsdp, 2), lax.div(fsdp, 2)


def device(y, z, core, x):
    return (z * 2 + y, x * 2 + core)


def greet(peers):
    barrier = pltpu.get_barrier_semaphore()
    for peer in peers:
        pl.semaphore_signal(barrier, inc=1, device_id=peer, device_id_type=MESH_ID)
    pl.semaphore_wait(barrier, len(peers))


def reduce_kernel(by_columns, *refs):
    count = len(by_columns)
    grads, gains = refs[:count], refs[count]
    outs, gain_out = refs[count + 1 : 2 * count + 1], refs[2 * count + 1]
    refs = refs[2 * count + 2 :]
    core_in, x_in, y_in, z_in = (refs[i * count : (i + 1) * count] for i in range(4))
    gain_in, gain_sum, send_sem, recv_sem, gain_send, gain_recv = refs[4 * count :]
    y, z, core, x = place()
    core_peer = device(y, z, 1 - core, x)
    x_peer = device(y, z, core, 1 - x)
    y_peer = device(1 - y, z, core, x)
    z_at = [lax.rem(z + hop, 4) for hop in (1, 2, 3)]
    z_peers = [device(y, other, core, x) for other in z_at]
    greet([core_peer, x_peer, y_peer] + z_peers)

    def quarter(item, ref, at):
        if by_columns[item]:
            width = ref.shape[1] // 4
            return ref.at[:, pl.ds(pl.multiple_of(at * width, 128), width)]
        width = ref.shape[0] // 4
        return ref.at[pl.ds(pl.multiple_of(at * width, 16), width), :]

    def copy(item, slot, source, target, peer):
        return pltpu.make_async_remote_copy(
            src_ref=source,
            dst_ref=target,
            send_sem=send_sem.at[item, slot],
            recv_sem=recv_sem.at[item, slot],
            device_id=peer,
            device_id_type=MESH_ID,
        )

    def gain_copy(slot, source, peer):
        return pltpu.make_async_remote_copy(
            src_ref=source,
            dst_ref=gain_in.at[slot],
            send_sem=gain_send.at[slot],
            recv_sem=gain_recv.at[slot],
            device_id=peer,
            device_id_type=MESH_ID,
        )

    def add_rows(target, others):
        rows = target.shape[0]

        @pl.loop(0, rows // 16)
        def _(step):
            span = pl.ds(pl.multiple_of(step * 16, 16), 16)
            total = others[0][span, :].astype(jnp.float32)
            for other in others[1:]:
                total = total + other[span, :].astype(jnp.float32)
            target[span, :] = total.astype(target.dtype)

    copies = [[None] * 10 for _ in range(count)]
    gain_copies = [None] * 6

    def stage_core(item):
        copies[item][0] = copy(item, 0, grads[item].at[:, 1 - core], core_in[item], core_peer)
        copies[item][0].start()

    def stage_x(item):
        copies[item][0].wait_recv()
        for side in range(2):
            for half in range(2):
                target = core_in[item].at[side, half]
                add_rows(target, [target, grads[item].at[side, core, half]])
        copies[item][1] = copy(item, 1, core_in[item].at[1 - x], x_in[item], x_peer)
        copies[item][1].start()

    def stage_y(item):
        copies[item][1].wait_recv()
        for half in range(2):
            target = x_in[item].at[half]
            add_rows(target, [target, core_in[item].at[x, half]])
        copies[item][2] = copy(item, 2, x_in[item].at[1 - y], y_in[item], y_peer)
        copies[item][2].start()

    def stage_z(item):
        copies[item][2].wait_recv()
        add_rows(y_in[item], [y_in[item], x_in[item].at[y]])
        for hop in range(3):
            copies[item][3 + hop] = copy(
                item, 3 + hop, quarter(item, y_in[item], z_at[hop]), z_in[item].at[hop], z_peers[hop]
            )
            copies[item][3 + hop].start()

    def stage_back_z(item):
        for hop in range(3):
            copies[item][3 + hop].wait_recv()
        mine = quarter(item, outs[item].at[y], z)
        add_rows(mine, [quarter(item, y_in[item], z)] + [z_in[item].at[hop] for hop in range(3)])
        for hop in range(3):
            copies[item][6 + hop] = copy(item, 6 + hop, mine, mine, z_peers[hop])
            copies[item][6 + hop].start()

    def stage_back_y(item):
        for hop in range(3):
            copies[item][6 + hop].wait_recv()
        copies[item][9] = copy(item, 9, outs[item].at[y], outs[item].at[y], y_peer)
        copies[item][9].start()

    def gain_step(step):
        if step == 0:
            gain_copies[0] = gain_copy(0, gains, core_peer)
            gain_copies[0].start()
        elif step <= 2:
            gain_copies[step - 1].wait_recv()
            before = gains if step == 1 else gain_sum.at[step - 2]
            gain_sum[step - 1] = before[...] + gain_in[step - 1]
            gain_copies[step] = gain_copy(step, gain_sum.at[step - 1], (x_peer, y_peer)[step - 1])
            gain_copies[step].start()
        elif step == 3:
            gain_copies[2].wait_recv()
            gain_sum[2] = gain_sum[1] + gain_in[2]
            for hop in range(3):
                gain_copies[3 + hop] = gain_copy(3 + hop, gain_sum.at[2], z_peers[hop])
                gain_copies[3 + hop].start()
        elif step == 4:
            for hop in range(3):
                gain_copies[3 + hop].wait_recv()
            gain_out[...] = (gain_sum[2] + gain_in[4]) + (gain_in[3] + gain_in[5])

    for item in range(count):
        stage_core(item)
    stages = (stage_x, stage_y, stage_z, stage_back_z, stage_back_y)
    for tick in range(count + len(stages) - 1):
        for at, stage in enumerate(stages):
            if 0 <= tick - at < count:
                stage(tick - at)
        gain_step(tick)
    for item in range(count):
        copies[item][9].wait_recv()
    for item in range(count):
        for slot in range(10):
            copies[item][slot].wait_send()
    for slot in range(6):
        gain_copies[slot].wait_send()


def reduce_all(grads, by_columns, gains):
    shaped, outs, scratch = [], [], [[], [], [], []]
    for grad, columns_split in zip(grads, by_columns):
        rows, columns = grad.shape[0] // 8, grad.shape[1]
        shaped.append(grad.reshape(2, 2, 2, rows, columns))
        outs.append(jax.ShapeDtypeStruct((2, rows, columns), jnp.bfloat16))
        piece = (rows, columns // 4) if columns_split else (rows // 4, columns)
        scratch[0].append(pltpu.VMEM((2, 2, rows, columns), jnp.bfloat16))
        scratch[1].append(pltpu.VMEM((2, rows, columns), jnp.bfloat16))
        scratch[2].append(pltpu.VMEM((rows, columns), jnp.bfloat16))
        scratch[3].append(pltpu.VMEM((3,) + piece, jnp.bfloat16))
    count = len(grads)
    outs.append(jax.ShapeDtypeStruct(gains.shape, jnp.float32))
    sent = sum(grad.size for grad in grads)

    def kernel(*refs):
        reduce_kernel(by_columns, *refs)

    results = pl.pallas_call(
        kernel,
        out_shape=outs,
        in_specs=[pl.BlockSpec(memory_space=pltpu.VMEM)] * (count + 1),
        out_specs=[pl.BlockSpec(memory_space=pltpu.VMEM)] * (count + 1),
        scratch_shapes=scratch[0]
        + scratch[1]
        + scratch[2]
        + scratch[3]
        + [
            pltpu.VMEM((6,) + gains.shape, jnp.float32),
            pltpu.VMEM((3,) + gains.shape, jnp.float32),
            pltpu.SemaphoreType.DMA((count, 10)),
            pltpu.SemaphoreType.DMA((count, 10)),
            pltpu.SemaphoreType.DMA((6,)),
            pltpu.SemaphoreType.DMA((6,)),
        ],
        compiler_params=pltpu.CompilerParams(
            collective_id=1, has_side_effects=True, vmem_limit_bytes=VMEM_BYTES
        ),
        cost_estimate=pl.CostEstimate(flops=2 * sent, bytes_accessed=4 * sent, transcendentals=0),
        name="reduce_grads",
    )(*shaped, gains)
    return [
        result.reshape(2 * result.shape[1], result.shape[2]) for result in results[:-1]
    ] + [results[-1]]


def gather_kernel(count, *refs):
    shards, outs = refs[:count], refs[count : 2 * count]
    send_sem, recv_sem, own_sem = refs[2 * count :]
    y, z, core, x = place()
    core_peer = device(y, z, 1 - core, x)
    x_peer = device(y, z, core, 1 - x)
    y_peer = device(1 - y, z, core, x)
    greet([core_peer, x_peer, y_peer])

    def send(item, slot, source, target, peer):
        copy = pltpu.make_async_remote_copy(
            src_ref=source,
            dst_ref=target,
            send_sem=send_sem.at[item, slot],
            recv_sem=recv_sem.at[item, slot],
            device_id=peer,
            device_id_type=MESH_ID,
        )
        copy.start()
        return copy

    copies = [[None] * 5 for _ in range(count)]
    for item in range(count):
        copies[item][1] = send(item, 1, shards[item].at[y], outs[item].at[x, core, y], x_peer)
    for item in range(count):
        copies[item][0] = send(item, 0, shards[item], outs[item].at[x, core], core_peer)
    own = [
        pltpu.make_async_copy(shards[item], outs[item].at[x, core], own_sem.at[item])
        for item in range(count)
    ]
    for copy in own:
        copy.start()
    for tick in range(count + 1):
        if tick < count:
            copies[tick][1].wait_recv()
            here = outs[tick].at[1 - x, core, y]
            copies[tick][2] = send(tick, 2, here, here, y_peer)
            copies[tick][3] = send(tick, 3, here, here, core_peer)
        if tick >= 1:
            copies[tick - 1][2].wait_recv()
            there = outs[tick - 1].at[1 - x, core, 1 - y]
            copies[tick - 1][4] = send(tick - 1, 4, there, there, core_peer)
    for item in range(count):
        own[item].wait()
        for slot in (0, 3, 4):
            copies[item][slot].wait_recv()
        for slot in range(5):
            copies[item][slot].wait_send()


def gather_all(shards):
    shaped = [item.reshape(2, item.shape[0] // 2, item.shape[1]) for item in shards]
    count = len(shards)
    sent = sum(item.size for item in shards)

    def kernel(*refs):
        gather_kernel(count, *refs)

    results = pl.pallas_call(
        kernel,
        out_shape=[jax.ShapeDtypeStruct((2, 2) + item.shape, item.dtype) for item in shaped],
        in_specs=[pl.BlockSpec(memory_space=pltpu.VMEM)] * count,
        out_specs=[pl.BlockSpec(memory_space=pltpu.VMEM)] * count,
        scratch_shapes=[
            pltpu.SemaphoreType.DMA((count, 5)),
            pltpu.SemaphoreType.DMA((count, 5)),
            pltpu.SemaphoreType.DMA((count,)),
        ],
        compiler_params=pltpu.CompilerParams(
            collective_id=2, has_side_effects=True, vmem_limit_bytes=VMEM_BYTES
        ),
        cost_estimate=pl.CostEstimate(flops=0, bytes_accessed=10 * sent, transcendentals=0),
        name="gather_weights",
    )(*shaped)
    return [
        result.reshape(4 * item.shape[0], item.shape[1]) for result, item in zip(results, shards)
    ]


def gather_fast(weights, gains):
    query, key, value, out, gate, up, down = weights
    wide = 256
    rows = [jnp.pad(gain, (0, wide - gain.shape[0])) for gain in gains]
    pack = jnp.pad(jnp.stack(rows), ((0, 16 - len(rows)), (0, 0)))
    joined, out, gate, up, down, packs = gather_all(
        [
            jnp.concatenate([query, key, value], axis=1),
            out,
            gate,
            up,
            down,
            jnp.concatenate([pack, pack], axis=0),
        ]
    )
    first, second = query.shape[1], query.shape[1] + key.shape[1]
    packs = packs.reshape(4, 2, 16, wide)
    whole_gains = [
        packs[:, 0, at, : gain.shape[0]].reshape(4 * gain.shape[0]) for at, gain in enumerate(gains)
    ]
    return (
        joined[:, :first],
        joined[:, first:second],
        joined[:, second:],
        out,
        gate,
        up,
        down,
        *whole_gains,
    )


def gelu_mix(gate_in, up_in):
    return jax.nn.gelu(gate_in, approximate=True) * up_in


def body(
    inputs,
    cotangent,
    lengths,
    query_weight,
    key_weight,
    value_weight,
    out_weight,
    gate_weight,
    up_weight,
    down_weight,
    pre_attn_gain,
    post_attn_gain,
    pre_ffw_gain,
    post_ffw_gain,
    query_gain,
    key_gain,
):
    seq_count, row_count, model_width = inputs.shape
    fast = lax.axis_size("ctx") == 8 and lax.axis_size("fsdp") == 4
    weights = (
        query_weight,
        key_weight,
        value_weight,
        out_weight,
        gate_weight,
        up_weight,
        down_weight,
    )
    gains = (
        pre_attn_gain,
        post_attn_gain,
        pre_ffw_gain,
        post_ffw_gain,
        query_gain,
        key_gain,
    )
    if fast:
        gathered = gather_fast(weights, gains)
    else:
        gathered = tuple(
            lax.all_gather(item, "fsdp", axis=0, tiled=True) for item in weights + gains
        )
    (
        query_full,
        key_full,
        value_full,
        out_full,
        gate_full,
        up_full,
        down_full,
        gain_attn_in,
        gain_attn_out,
        gain_ffw_in,
        gain_ffw_out,
        gain_query,
        gain_key,
    ) = gathered
    gain_attn_in = gain_attn_in.astype(jnp.float32)
    gain_attn_out = gain_attn_out.astype(jnp.float32)
    gain_ffw_in = gain_ffw_in.astype(jnp.float32)
    gain_ffw_out = gain_ffw_out.astype(jnp.float32)
    gain_query = gain_query.astype(jnp.float32)
    gain_key = gain_key.astype(jnp.float32)
    head_dim = key_full.shape[1]
    head_count = query_full.shape[1] // head_dim
    seq_len = row_count * lax.axis_size("ctx")
    key_span = math.gcd(512, seq_len)
    att_scale = head_dim ** (-0.5)
    flat_rows = seq_count * row_count
    positions = lax.axis_index("ctx") * row_count + jnp.arange(row_count, dtype=jnp.int32)
    x_flat = inputs.astype(jnp.float32).reshape(flat_rows, model_width)
    attn_in, attn_in_back = jax.vjp(norm_gain, x_flat, gain_attn_in)
    attn_in_b = attn_in.astype(jnp.bfloat16)
    query_lin = jnp.dot(attn_in_b, query_full, preferred_element_type=jnp.float32)
    key_lin = jnp.dot(attn_in_b, key_full, preferred_element_type=jnp.float32)
    value_lin = jnp.dot(attn_in_b, value_full, preferred_element_type=jnp.float32)

    def query_side(lin_values, gain_vec):
        return rotate(
            norm_gain(lin_values.reshape(seq_count, row_count, head_count, head_dim), gain_vec),
            positions,
        )

    def key_side(lin_values, gain_vec):
        return rotate(
            norm_gain(lin_values.reshape(seq_count, row_count, 1, head_dim), gain_vec), positions
        )[:, :, 0, :]

    query_rot, query_side_back = jax.vjp(query_side, query_lin, gain_query)
    key_rot, key_side_back = jax.vjp(key_side, key_lin, gain_key)
    query_b = query_rot.astype(jnp.bfloat16)
    key_b = key_rot.astype(jnp.bfloat16)
    value_b = value_lin.reshape(seq_count, row_count, head_dim).astype(jnp.bfloat16)

    def allowed(key_begin, key_count):
        key_pos = key_begin + jnp.arange(key_count, dtype=jnp.int32)
        causal = key_pos[None, :] <= positions[:, None]
        live = key_pos[None, :] < lengths[:, None]
        return (causal[None] & live[:, None, :])[:, None]

    def raw_scores(key_piece):
        return (
            jnp.einsum("sqhd,skd->shqk", query_b, key_piece, preferred_element_type=jnp.float32)
            * att_scale
        )

    stat_shape = (seq_count, head_count, row_count)
    running_max = jnp.full(stat_shape, MASKED_SCORE, jnp.float32)
    both = lax.all_gather(jnp.concatenate([key_b, value_b], axis=-1), "ctx", axis=1, tiled=True)
    key_piece, value_piece = both[..., :head_dim], both[..., head_dim:]
    mask_now = allowed(jnp.int32(0), key_piece.shape[1])
    scores = jnp.where(mask_now, raw_scores(key_piece), MASKED_SCORE)
    new_max = jnp.maximum(running_max, jnp.max(scores, axis=-1))
    weights = jnp.where(mask_now, jnp.exp(scores - new_max[..., None]), 0.0)
    new_sum = jnp.sum(weights, axis=-1)
    new_acc = jnp.einsum(
        "shqk,skd->shqd",
        weights.astype(jnp.bfloat16),
        value_piece,
        preferred_element_type=jnp.float32,
    )
    final_state = (new_max, new_sum, new_acc)
    final_max, final_sum, final_acc = final_state
    attended = final_acc / final_sum[..., None]
    log_total = final_max + jnp.log(final_sum)
    attended_b = (
        attended.transpose(0, 2, 1, 3)
        .reshape(flat_rows, head_count * head_dim)
        .astype(jnp.bfloat16)
    )
    attn_lin = jnp.dot(attended_b, out_full, preferred_element_type=jnp.float32)
    attn_post, attn_post_back = jax.vjp(norm_gain, attn_lin, gain_attn_out)
    middle = x_flat + attn_post
    ffw_in, ffw_in_back = jax.vjp(norm_gain, middle, gain_ffw_in)
    ffw_in_b = ffw_in.astype(jnp.bfloat16)
    gate_lin = jnp.dot(ffw_in_b, gate_full, preferred_element_type=jnp.float32)
    up_lin = jnp.dot(ffw_in_b, up_full, preferred_element_type=jnp.float32)
    hidden, hidden_back = jax.vjp(gelu_mix, gate_lin, up_lin)
    hidden_b = hidden.astype(jnp.bfloat16)
    ffw_out = jnp.dot(hidden_b, down_full, preferred_element_type=jnp.float32)
    ffw_post, ffw_post_back = jax.vjp(norm_gain, ffw_out, gain_ffw_out)
    outputs = (middle + ffw_post).astype(jnp.bfloat16).reshape(seq_count, row_count, model_width)
    grad_top = cotangent.astype(jnp.float32).reshape(flat_rows, model_width)
    d_ffw_out, grad_ffw_out_gain = ffw_post_back(grad_top)
    d_ffw_out_b = d_ffw_out.astype(jnp.bfloat16)
    grad_down = jnp.einsum("rf,rd->fd", hidden_b, d_ffw_out_b, preferred_element_type=jnp.float32)
    d_hidden = jnp.einsum("rd,fd->rf", d_ffw_out_b, down_full, preferred_element_type=jnp.float32)
    d_gate, d_up = hidden_back(d_hidden)
    d_gate_b = d_gate.astype(jnp.bfloat16)
    d_up_b = d_up.astype(jnp.bfloat16)
    grad_gate = jnp.einsum("rd,rf->df", ffw_in_b, d_gate_b, preferred_element_type=jnp.float32)
    grad_up = jnp.einsum("rd,rf->df", ffw_in_b, d_up_b, preferred_element_type=jnp.float32)
    d_ffw_in = jnp.einsum(
        "rf,df->rd", d_gate_b, gate_full, preferred_element_type=jnp.float32
    ) + jnp.einsum("rf,df->rd", d_up_b, up_full, preferred_element_type=jnp.float32)
    d_middle_part, grad_ffw_in_gain = ffw_in_back(d_ffw_in)
    d_middle = grad_top + d_middle_part
    d_attn_lin, grad_attn_out_gain = attn_post_back(d_middle)
    d_attn_b = d_attn_lin.astype(jnp.bfloat16)
    grad_projection = jnp.einsum(
        "ro,rd->od", attended_b, d_attn_b, preferred_element_type=jnp.float32
    )
    d_attended_b = (
        jnp.einsum("rd,od->ro", d_attn_b, out_full, preferred_element_type=jnp.float32)
        .astype(jnp.bfloat16)
        .reshape(seq_count, row_count, head_count, head_dim)
    )
    d_attended = d_attended_b.astype(jnp.float32)
    row_delta = jnp.einsum("sqhd,shqd->shq", d_attended, attended, precision=lax.Precision.HIGHEST)

    def key_grads(key_piece, value_piece, key_begin):
        mask_now = allowed(key_begin, key_piece.shape[1])
        probabilities = jnp.where(
            mask_now, jnp.exp(raw_scores(key_piece) - log_total[..., None]), 0.0
        )
        d_probs = jnp.einsum(
            "sqhd,skd->shqk", d_attended_b, value_piece, preferred_element_type=jnp.float32
        )
        d_scores = (probabilities * (d_probs - row_delta[..., None])).astype(jnp.bfloat16)
        d_query = (
            jnp.einsum("shqk,skd->sqhd", d_scores, key_piece, preferred_element_type=jnp.float32)
            * att_scale
        )
        d_key = (
            jnp.einsum("shqk,sqhd->skd", d_scores, query_b, preferred_element_type=jnp.float32)
            * att_scale
        )
        d_value = jnp.einsum(
            "shqk,sqhd->skd",
            probabilities.astype(jnp.bfloat16),
            d_attended_b,
            preferred_element_type=jnp.float32,
        )
        return (d_query, jnp.concatenate([d_key, d_value], axis=-1))

    key_back_all, value_back_all = key_piece, value_piece

    def slice_keys(key_begin, key_count):
        return (
            lax.dynamic_slice_in_dim(key_back_all, key_begin, key_count, 1),
            lax.dynamic_slice_in_dim(value_back_all, key_begin, key_count, 1),
        )

    query_zero = jnp.zeros((seq_count, row_count, head_count, head_dim), jnp.float32)

    def joint_step(block_id, state):
        d_query_sum, key_buffer = state
        key_begin = block_id * key_span
        key_piece, value_piece = slice_keys(key_begin, key_span)
        d_query, d_keyval = key_grads(key_piece, value_piece, key_begin)
        return (
            d_query_sum + d_query,
            lax.dynamic_update_slice_in_dim(key_buffer, d_keyval, key_begin, 1),
        )

    if seq_len <= 1024:
        d_query_rot, key_buffer = key_grads(key_back_all, value_back_all, jnp.int32(0))
    else:
        d_query_rot, key_buffer = lax.fori_loop(
            0,
            seq_len // key_span,
            joint_step,
            (query_zero, jnp.zeros((seq_count, seq_len, 2 * head_dim), jnp.float32)),
        )
    d_keyval_own = lax.psum_scatter(
        key_buffer.astype(jnp.bfloat16), "ctx", scatter_dimension=1, tiled=True
    ).astype(jnp.float32)
    d_key_rot = d_keyval_own[..., :head_dim]
    d_value = d_keyval_own[..., head_dim:]
    d_query_lin, grad_query_gain = query_side_back(d_query_rot)
    d_key_lin, grad_key_gain = key_side_back(d_key_rot)
    d_query_b = d_query_lin.astype(jnp.bfloat16)
    d_key_b = d_key_lin.astype(jnp.bfloat16)
    d_value_b = d_value.reshape(flat_rows, head_dim).astype(jnp.bfloat16)
    grad_query = jnp.einsum("rd,rq->dq", attn_in_b, d_query_b, preferred_element_type=jnp.float32)
    grad_key = jnp.einsum("rd,rq->dq", attn_in_b, d_key_b, preferred_element_type=jnp.float32)
    grad_value = jnp.einsum("rd,rq->dq", attn_in_b, d_value_b, preferred_element_type=jnp.float32)
    d_attn_in = jnp.einsum("rq,dq->rd", d_query_b, query_full, preferred_element_type=jnp.float32)
    d_attn_in = d_attn_in + jnp.einsum(
        "rq,dq->rd", d_key_b, key_full, preferred_element_type=jnp.float32
    )
    d_attn_in = d_attn_in + jnp.einsum(
        "rq,dq->rd", d_value_b, value_full, preferred_element_type=jnp.float32
    )
    d_input_part, grad_attn_in_gain = attn_in_back(d_attn_in)
    input_grad = (
        (d_middle + d_input_part).astype(jnp.bfloat16).reshape(seq_count, row_count, model_width)
    )
    if fast:
        gain_rows = [
            grad_attn_in_gain,
            grad_attn_out_gain,
            grad_ffw_in_gain,
            grad_ffw_out_gain,
            jnp.pad(grad_query_gain, (0, model_width - head_dim)),
            jnp.pad(grad_key_gain, (0, model_width - head_dim)),
        ]
        gain_pack = jnp.pad(jnp.stack(gain_rows), ((0, 2), (0, 0)))
        grads_in = jnp.concatenate([grad_query, grad_key, grad_value], axis=1)
        t_down, t_gate, t_up, t_projection, t_in, gain_totals = reduce_all(
            [
                grad_down.astype(jnp.bfloat16),
                grad_gate.astype(jnp.bfloat16),
                grad_up.astype(jnp.bfloat16),
                grad_projection.astype(jnp.bfloat16),
                grads_in.astype(jnp.bfloat16),
            ],
            (False, True, True, False, True),
            gain_pack,
        )
        part = lax.axis_index("fsdp")
        wide = head_count * head_dim
        results = [
            t_in[:, :wide],
            t_in[:, wide : wide + head_dim],
            t_in[:, wide + head_dim :],
            t_projection,
            t_gate,
            t_up,
            t_down,
        ]
        results = [item.astype(jnp.float32) for item in results]
        for at in range(6):
            size = (model_width if at < 4 else head_dim) // 4
            results.append(lax.dynamic_slice_in_dim(gain_totals[at], part * size, size, 0))
        return (outputs, input_grad) + tuple(results)
    shards = (
        lax.psum_scatter(
            grad_query.astype(jnp.bfloat16), "fsdp", scatter_dimension=0, tiled=True
        ).astype(jnp.float32),
        lax.psum_scatter(
            grad_key.astype(jnp.bfloat16), "fsdp", scatter_dimension=0, tiled=True
        ).astype(jnp.float32),
        lax.psum_scatter(
            grad_value.astype(jnp.bfloat16), "fsdp", scatter_dimension=0, tiled=True
        ).astype(jnp.float32),
        lax.psum_scatter(
            grad_projection.astype(jnp.bfloat16), "fsdp", scatter_dimension=0, tiled=True
        ).astype(jnp.float32),
        lax.psum_scatter(
            grad_gate.astype(jnp.bfloat16), "fsdp", scatter_dimension=0, tiled=True
        ).astype(jnp.float32),
        lax.psum_scatter(
            grad_up.astype(jnp.bfloat16), "fsdp", scatter_dimension=0, tiled=True
        ).astype(jnp.float32),
        lax.psum_scatter(
            grad_down.astype(jnp.bfloat16), "fsdp", scatter_dimension=0, tiled=True
        ).astype(jnp.float32),
        lax.psum_scatter(
            grad_attn_in_gain.astype(jnp.bfloat16), "fsdp", scatter_dimension=0, tiled=True
        ).astype(jnp.float32),
        lax.psum_scatter(
            grad_attn_out_gain.astype(jnp.bfloat16), "fsdp", scatter_dimension=0, tiled=True
        ).astype(jnp.float32),
        lax.psum_scatter(
            grad_ffw_in_gain.astype(jnp.bfloat16), "fsdp", scatter_dimension=0, tiled=True
        ).astype(jnp.float32),
        lax.psum_scatter(
            grad_ffw_out_gain.astype(jnp.bfloat16), "fsdp", scatter_dimension=0, tiled=True
        ).astype(jnp.float32),
        lax.psum_scatter(
            grad_query_gain.astype(jnp.bfloat16), "fsdp", scatter_dimension=0, tiled=True
        ).astype(jnp.float32),
        lax.psum_scatter(
            grad_key_gain.astype(jnp.bfloat16), "fsdp", scatter_dimension=0, tiled=True
        ).astype(jnp.float32),
    )
    totals = lax.psum(
        (
            shards[0],
            shards[1],
            shards[2],
            shards[3],
            shards[4],
            shards[5],
            shards[6],
            shards[7],
            shards[8],
            shards[9],
            shards[10],
            shards[11],
            shards[12],
        ),
        "ctx",
    )
    return (outputs, input_grad) + tuple(totals)


def solution(mesh):
    in_specs = (
        P("fsdp", "ctx", None),
        P("fsdp", "ctx", None),
        P("fsdp"),
        P("fsdp", None),
        P("fsdp", None),
        P("fsdp", None),
        P("fsdp", None),
        P("fsdp", None),
        P("fsdp", None),
        P("fsdp", None),
        P("fsdp"),
        P("fsdp"),
        P("fsdp"),
        P("fsdp"),
        P("fsdp"),
        P("fsdp"),
    )
    out_specs = (
        P("fsdp", "ctx", None),
        P("fsdp", "ctx", None),
        P("fsdp", None),
        P("fsdp", None),
        P("fsdp", None),
        P("fsdp", None),
        P("fsdp", None),
        P("fsdp", None),
        P("fsdp", None),
        P("fsdp"),
        P("fsdp"),
        P("fsdp"),
        P("fsdp"),
        P("fsdp"),
        P("fsdp"),
    )
    return jax.shard_map(body, mesh=mesh, in_specs=in_specs, out_specs=out_specs, check_vma=False)
```
